32 devices in a mesh: grp: 2 (over x), seq: 16 (over z, y, core).
Axes of the slice: x: 2, y: 2, z: 4, core: 2. Of those that a mesh axis runs over, the one named last changes fastest.
Arguments:
- queries: bfloat16 [2, 2048, 4608], P('grp', 'seq'), may hold values from -16 to 16
- latents: bfloat16 [2, 2048, 576], P('grp', 'seq'), may hold values from -6 to 6
- cotangent: bfloat16 [2, 2048, 4096], P('grp', 'seq'), may hold values from -6 to 6
- comp_weight: float32 [32, 576], replicated, may hold values from -1 to 1
- sel_idx: int32 [2, 32, 64], P('grp', 'seq'), may hold values from 0 to 63, as said below
- sel_count: int32 [2, 32], P('grp', 'seq'), may hold values from 0 to 62, as said below
Outputs:
- attended: bfloat16 [2, 2048, 4096], P('grp', 'seq')
- query_grads: bfloat16 [2, 2048, 4608], P('grp', 'seq')
- latent_grads: float32 [2, 2048, 576], P('grp', 'seq')
- comp_weight_grads: float32 [32, 576], replicated
The draws below stay inside these ranges and needn't reach their ends.
Inputs may be any that keep to these rules, and one draw needn't show every extreme that they name: `sel_idx`: in query block r the first sel_count entries are distinct compressed-latent numbers below r * 2; the other entries are 0 and unused. sel_count of query block r is at most min(64, r * 2); the last query block of every sequence reaches min(64, 62).
All inputs are finite; a program needn't handle non-finite values.
Results may differ from the reference program's by a relative error of at most 0.019.
Values may be sent and summed in bfloat16 or wider, within the bound.
A program may use at most 64 MiB of HBM per device.

```python
import jax
import jax.numpy as jnp
from jax import lax

DL = 512
DR = 64
H = 8
QB = 64
CS = 32
SEL = 64
WIN = 512
DK = 576
GROUPS = 2
TOKENS = 2048
NCMP = 64
NQB = 32


def joint_fields(key):
    key_latent = jax.random.fold_in(key, 11)
    key_query = jax.random.fold_in(key, 12)
    latent_field = jnp.clip(jax.random.normal(key_latent, (GROUPS, TOKENS, DK), jnp.float32), -6.0, 6.0)
    query_field = jnp.clip(jax.random.normal(key_query, (GROUPS, TOKENS, H, DK), jnp.float32), -6.0, 6.0)
    return (latent_field, query_field)


def draw_queries(key, part):
    latent_field, query_field = joint_fields(key)
    return query_field.reshape(GROUPS, TOKENS, H * DK).astype(jnp.bfloat16)


def draw_latents(key, part):
    latent_field, query_field = joint_fields(key)
    return latent_field.astype(jnp.bfloat16)


def selection(key):
    key_order = jax.random.fold_in(key, 21)
    key_count = jax.random.fold_in(key, 22)
    block_ids = jnp.arange(NQB, dtype=jnp.int32)
    available = block_ids * (QB // CS)
    candidate = jnp.arange(NCMP, dtype=jnp.int32)
    random_ranks = jax.random.randint(key_order, (GROUPS, NQB, NCMP), 0, NCMP, dtype=jnp.int32)
    barred = jnp.where(candidate[None, :] >= available[:, None], NCMP * NCMP, 0).astype(jnp.int32)
    ranking = random_ranks * NCMP + candidate[None, None, :] + barred[None]
    ranked = jnp.argsort(ranking, axis=2, stable=True)[:, :, :SEL].astype(jnp.int32)
    wanted = jax.random.randint(key_count, (GROUPS, NQB), SEL // 2, SEL + 1, dtype=jnp.int32)
    wanted = jnp.where(block_ids[None, :] == NQB - 1, SEL, wanted)
    live_count = jnp.minimum(wanted, available[None, :]).astype(jnp.int32)
    slot_ids = jnp.arange(SEL, dtype=jnp.int32)
    chosen_ids = jnp.where(slot_ids[None, None, :] < live_count[:, :, None], ranked, 0).astype(jnp.int32)
    return (chosen_ids, live_count)


def draw_sel_idx(key, part):
    chosen_ids, live_count = selection(key)
    return chosen_ids


def draw_sel_count(key, part):
    chosen_ids, live_count = selection(key)
    return live_count


def steps_of(key, shape, cuts, smallest, largest):
    def one(dim, shards_of):
        draws = jax.random.uniform(jax.random.fold_in(jax.random.fold_in(key, 6), dim), (shards_of,), jnp.float32, smallest / len(cuts), largest / len(cuts))
        return jnp.repeat(jnp.exp(draws), shape[dim] // shards_of).reshape((-1,) + (1,) * (len(shape) - dim - 1))

    loudness = one(*cuts[0])
    for cut in cuts[1:]:
        loudness = loudness * one(*cut)
    return loudness


def scatter_about(own_key, shape, deviation, most, pieces=(), kind=jnp.bfloat16):
    array = jax.random.normal(own_key, shape, jnp.float32) * deviation
    if len(pieces) > 0:
        array = steps_of(own_key, shape, pieces, -0.22, 0.18) * array
    return jnp.clip(array, min=-most, max=most).astype(kind)


def setup_inputs(seed: int = 0) -> dict:
    key_of = jax.random.split(jax.random.key(seed), 7)
    return {
        "queries": draw_queries(jax.random.fold_in(key_of[6], 71), 0),
        "latents": draw_latents(jax.random.fold_in(key_of[6], 71), 0),
        "cotangent": scatter_about(key_of[2], (GROUPS, TOKENS, H * DL), 1.0, 6.0, ((0, 2), (1, 16))),
        "comp_weight": scatter_about(key_of[3], (CS, DK), CS ** -0.5, 1.0, (), jnp.float32),
        "sel_idx": draw_sel_idx(jax.random.fold_in(key_of[6], 71), 0),
        "sel_count": draw_sel_count(jax.random.fold_in(key_of[6], 71), 0),
    }


score_scale = 192.0 ** -0.5


def forward_block(query_rows, grad_rows, key_rows, allowed):
    scores = jnp.einsum("qhd,kd->qhk", query_rows.astype(jnp.float32), key_rows.astype(jnp.float32)) * score_scale
    scores = jnp.where(allowed[:, None, :], scores, -jnp.inf)
    row_max = jnp.max(scores, axis=2, keepdims=True)
    expo_part = jnp.exp(scores - row_max)
    row_sum = jnp.sum(expo_part, axis=2, keepdims=True)
    weights = expo_part / row_sum
    rounded = weights.astype(jnp.bfloat16)
    value_rows = key_rows[:, :DL]
    context = jnp.einsum("qhk,kd->qhd", rounded.astype(jnp.float32), value_rows.astype(jnp.float32))
    prob_grad = jnp.einsum("qhd,kd->qhk", grad_rows.astype(jnp.float32), value_rows.astype(jnp.float32))
    row_dot = jnp.sum(grad_rows.astype(jnp.float32) * context, axis=2, keepdims=True)
    dscore = (weights * (prob_grad - row_dot)).astype(jnp.bfloat16)
    query_grad = jnp.einsum("qhk,kd->qhd", dscore.astype(jnp.float32), key_rows.astype(jnp.float32)) * score_scale
    return context, query_grad, dscore, rounded


def key_terms(query_rows, grad_rows, dscore, rounded):
    key_grad = jnp.einsum("qhk,qhd->kd", dscore.astype(jnp.float32), query_rows.astype(jnp.float32)) * score_scale
    value_grad = jnp.einsum("qhk,qhd->kd", rounded.astype(jnp.float32), grad_rows.astype(jnp.float32))
    return key_grad + jnp.pad(value_grad, ((0, 0), (0, DR)))


def reference(queries, latents, cotangent, comp_weight, sel_idx, sel_count):
    slot_ids = jnp.arange(SEL, dtype=jnp.int32)
    offsets = jnp.arange(WIN + QB, dtype=jnp.int32)
    within = jnp.arange(QB, dtype=jnp.int32)

    def one_group(inputs):
        group_queries, group_latents, group_grad, group_idx, group_count = inputs
        query_all = group_queries.reshape(TOKENS, H, DK)
        grad_all = group_grad.reshape(TOKENS, H, DL)
        block_view = group_latents.astype(jnp.float32).reshape(NCMP, CS, DK)
        compressed = jnp.sum(block_view * comp_weight[None], axis=1).astype(jnp.bfloat16)
        padded = jnp.concatenate([jnp.zeros((WIN, DK), jnp.bfloat16), group_latents], axis=0)

        def block_step(state_pair, block_id):
            padded_grad, compressed_grad = state_pair
            first_row = (block_id * QB).astype(jnp.int32)
            query_rows = lax.dynamic_slice_in_dim(query_all, first_row, QB, 0)
            grad_rows = lax.dynamic_slice_in_dim(grad_all, first_row, QB, 0)
            window_rows = lax.dynamic_slice_in_dim(padded, first_row, WIN + QB, 0)
            chosen = group_idx[block_id]
            live_slots = slot_ids < group_count[block_id]
            picked = jnp.take(compressed, chosen, axis=0)
            query_pos = first_row + within
            key_pos = first_row - WIN + offsets
            window_ok = (key_pos[None, :] <= query_pos[:, None]) & (key_pos[None, :] > query_pos[:, None] - WIN) & (key_pos[None, :] >= 0)
            allowed = jnp.concatenate([jnp.broadcast_to(live_slots[None, :], (QB, SEL)), window_ok], axis=1)
            key_rows = jnp.concatenate([picked, window_rows], axis=0)
            context, query_grad, dscore, rounded = forward_block(query_rows, grad_rows, key_rows, allowed)
            key_grad = key_terms(query_rows, grad_rows, dscore, rounded)
            compressed_grad = compressed_grad.at[chosen].add(key_grad[:SEL] * live_slots[:, None].astype(jnp.float32))
            old_rows = lax.dynamic_slice_in_dim(padded_grad, first_row, WIN + QB, 0)
            padded_grad = lax.dynamic_update_slice_in_dim(padded_grad, old_rows + key_grad[SEL:], first_row, 0)
            return (padded_grad, compressed_grad), (context.astype(jnp.bfloat16), query_grad.astype(jnp.bfloat16))

        initial = (jnp.zeros((TOKENS + WIN, DK), jnp.float32), jnp.zeros((NCMP, DK), jnp.float32))
        (padded_grad, compressed_grad), (contexts, query_grads) = lax.scan(block_step, initial, jnp.arange(NQB, dtype=jnp.int32))
        latent_grad = padded_grad[WIN:] + (comp_weight[None] * compressed_grad[:, None, :]).reshape(TOKENS, DK)
        weight_grad = jnp.sum(compressed_grad[:, None, :] * block_view, axis=0)
        return contexts.reshape(TOKENS, H * DL), query_grads.reshape(TOKENS, H * DK), latent_grad, weight_grad

    attended, query_grads, latent_grads, weight_grads = lax.map(one_group, (queries, latents, cotangent, sel_idx, sel_count))
    return attended, query_grads, latent_grads, jnp.sum(weight_grads, axis=0)
```

```python
import functools

import jax
import jax.numpy as jnp
from jax import lax
from jax.experimental import pallas as pl
from jax.experimental.pallas import tpu as pltpu
from jax.sharding import PartitionSpec as P

DL = 512
DR = 64
H = 8
QB = 64
CS = 32
WIN = 512
DK = 576
LANES = 128
WIDE = 640
PIECES = WIDE // LANES
SLOT = 8
MASKED = -1e30

MESH = pl.DeviceIdType.MESH
BF16 = jnp.bfloat16
F32 = jnp.float32
score_scale = 192.0 ** (-0.5)


def round_up(value, step):
    return (value + step - 1) // step * step


def dot_nn(a, b):
    return lax.dot_general(a, b, (((1,), (0,)), ((), ())), preferred_element_type=F32)


def dot_nt(a, b):
    return lax.dot_general(a, b, (((1,), (1,)), ((), ())), preferred_element_type=F32)


def dot_tn(a, b):
    return lax.dot_general(a, b, (((0,), (0,)), ((), ())), preferred_element_type=F32)


def piece_width(j):
    return min(LANES, DK - j * LANES)


def gather_kernel(n, hop, tok, cl, lat_ref, cw_ref, win_ref, comp_ref, tmp, wsend, wrecv, csend, crecv):
    seq = lax.axis_index("seq")
    grp = lax.axis_index("grp")
    barrier = pltpu.get_barrier_semaphore()

    def greet(k, c):
        pl.semaphore_signal(
            barrier, inc=1, device_id=(grp, lax.rem(seq + k, n)), device_id_type=MESH
        )
        return c

    lax.fori_loop(1, n, greet, 0)

    tmp[...] = jnp.zeros_like(tmp)
    for b in range(cl):
        block = lat_ref[pl.ds(b * CS, CS), :].astype(F32) * cw_ref[...]
        row = jnp.sum(block, axis=0, keepdims=True)
        for j in range(PIECES):
            w = piece_width(j)
            tmp[pl.ds(j * cl + b, 1), pl.ds(0, w)] = row[:, j * LANES : j * LANES + w]
    comp_ref[seq] = tmp[...].astype(BF16)
    pl.semaphore_wait(barrier, n - 1)

    def comp_copy(peer):
        return pltpu.make_async_remote_copy(
            src_ref=comp_ref.at[seq],
            dst_ref=comp_ref.at[seq],
            send_sem=csend.at[peer],
            recv_sem=crecv.at[seq],
            device_id=(grp, peer),
            device_id_type=MESH,
        )

    def comp_arrival(peer):
        return pltpu.make_async_remote_copy(
            src_ref=comp_ref.at[peer],
            dst_ref=comp_ref.at[peer],
            send_sem=csend.at[peer],
            recv_sem=crecv.at[peer],
            device_id=(grp, peer),
            device_id_type=MESH,
        )

    def win_copy(d):
        return pltpu.make_async_remote_copy(
            src_ref=lat_ref,
            dst_ref=win_ref.at[pl.ds((hop - d) * tok, tok)],
            send_sem=wsend.at[d],
            recv_sem=wrecv.at[d],
            device_id=(grp, lax.rem(seq + d, n)),
            device_id_type=MESH,
        )

    for d in range(1, hop + 1):
        pl.when(seq + d < n)(lambda d=d: win_copy(d).start())

    def send_comp(k, c):
        comp_copy(lax.rem(seq + k, n)).start()
        return c

    lax.fori_loop(1, n, send_comp, 0)
    for d in range(1, hop + 1):

        @pl.when(seq < d)
        def _(d=d):
            win_ref[pl.ds((hop - d) * tok, tok), :] = jnp.zeros((tok, DK), BF16)

    def wait_comp(k, c):
        comp_arrival(lax.rem(seq + k, n)).wait_recv()
        comp_copy(lax.rem(seq + k, n)).wait_send()
        return c

    lax.fori_loop(1, n, wait_comp, 0)
    for d in range(1, hop + 1):
        pl.when(seq >= d)(lambda d=d: win_copy(d).wait_recv())
        pl.when(seq + d < n)(lambda d=d: win_copy(d).wait_send())


def attend_kernel(
    n, hop, tok, cl,
    q_ref, cot_ref, lat_ref, win_ref, comp_ref, idx_ref, cnt_ref,
    att_ref, qg_ref, wing_ref, own_ref, cg_ref,
    kk, kf, qq, cc, bias, ds_ref, pp, dq, pack,
):
    cp = bias.shape[1] - round_up(hop * tok + tok, LANES)
    nk = bias.shape[1]
    lead = hop * tok
    ext = lead + tok
    half = (H // 2) * tok
    pair = 2 * DK
    seq = lax.axis_index("seq")
    pr = pack.shape[1]

    kf[pl.ds(0, cp), :] = jnp.zeros((cp, WIDE), F32)

    def unpack(o, c):
        packed = comp_ref[o].astype(F32)
        for j in range(PIECES):
            kf[pl.ds(pl.multiple_of(o * SLOT, SLOT), cl), pl.ds(j * LANES, LANES)] = packed[
                j * cl : (j + 1) * cl, :
            ]
        return c

    lax.fori_loop(0, n, unpack, 0)
    kf[pl.ds(cp, ext), pl.ds(DL, LANES)] = jnp.zeros((ext, LANES), F32)
    kf[pl.ds(cp, lead), pl.ds(0, DK)] = win_ref[...].astype(F32)
    kf[pl.ds(cp + lead, tok), pl.ds(0, DK)] = lat_ref[...].astype(F32)
    if nk > cp + ext:
        kf[pl.ds(cp + ext, nk - cp - ext), :] = jnp.zeros((nk - cp - ext, WIDE), F32)
    kk[0] = kf[...].astype(BF16)
    kk[1] = pltpu.roll(kf[...], DR, 1).astype(BF16)

    for m in range(H // 2):
        for p in range(2):
            rows = pl.ds(p * half + m * tok, tok)
            qq[rows, :] = q_ref[:, pl.ds(m * pair + p * DL, WIDE)]
            cc[rows, :] = cot_ref[:, pl.ds((2 * m + p) * DL, DL)]

    blocks = tok // QB
    slots = idx_ref.shape[1]
    key_id = lax.broadcasted_iota(jnp.int32, (cp, slots), 0)
    in_slot = key_id % SLOT
    comp_id = jnp.where(in_slot < cl, (key_id // SLOT) * cl + in_slot, -1)
    slot_id = lax.broadcasted_iota(jnp.int32, (cp, slots), 1)
    for r in range(blocks):
        chosen = idx_ref[pl.ds(r, 1), :]
        hit = (comp_id == chosen) & (slot_id < cnt_ref[0, r])
        hit = jnp.where(hit, 1.0, 0.0).astype(BF16)
        count = dot_nt(jnp.ones((QB, slots), BF16), hit)
        bias[pl.ds(r * QB, QB), pl.ds(0, cp)] = jnp.where(count > 0.5, 0.0, MASKED)
    wide = nk - cp
    row = lax.broadcasted_iota(jnp.int32, (tok, wide), 0)
    col = lax.broadcasted_iota(jnp.int32, (tok, wide), 1)
    shift = lead - WIN
    ok = (col > row + shift) & (col <= row + lead) & (col - lead + seq * tok >= 0)
    bias[:, pl.ds(cp, wide)] = jnp.where(ok, 0.0, MASKED)

    step = min(256, half)
    heads = step // tok
    for c in range(2 * half // step):
        p = c * step // half
        rows = pl.ds(c * step, step)
        keys = kk[p]
        values = kk[0, :, pl.ds(0, DL)]
        s = dot_nt(qq[rows, :], keys) * score_scale
        s = (s.reshape(heads, tok, nk) + bias[...][None]).reshape(step, nk)
        e = jnp.exp(s - jnp.max(s, axis=1, keepdims=True))
        w = e * (1.0 / jnp.sum(e, axis=1, keepdims=True))
        rounded = w.astype(BF16)
        pp[rows, :] = rounded
        context = dot_nn(rounded, values)
        grads = cc[rows, :]
        row_dot = jnp.sum(grads.astype(F32) * context, axis=1, keepdims=True)
        dscore = (w * (dot_nt(grads, values) - row_dot)).astype(BF16)
        ds_ref[rows, :] = dscore
        dq[rows, :] = dot_nn(dscore, keys) * score_scale
        for i in range(heads):
            m = (c * step - p * half) // tok + i
            att_ref[:, pl.ds((2 * m + p) * DL, DL)] = context[i * tok : (i + 1) * tok].astype(BF16)

    for m in range(H // 2):
        even = pl.ds(m * tok, tok)
        odd = pl.ds(half + m * tok, tok)
        qg_ref[:, pl.ds(m * pair, DL)] = dq[even, pl.ds(0, DL)].astype(BF16)
        qg_ref[:, pl.ds(m * pair + DL, LANES)] = (
            dq[even, pl.ds(DL, LANES)] + dq[odd, pl.ds(0, LANES)]
        ).astype(BF16)
        qg_ref[:, pl.ds(m * pair + WIDE, DL)] = dq[odd, pl.ds(LANES, DL)].astype(BF16)

    for start in range(0, nk, 256):
        size = min(256, nk - start)
        cols = pl.ds(start, size)
        even = dot_tn(ds_ref[pl.ds(0, half), cols], qq[pl.ds(0, half), :])
        odd = dot_tn(ds_ref[pl.ds(half, half), cols], qq[pl.ds(half, half), :])
        value = dot_tn(pp[:, cols], cc[...])
        total = (even + pltpu.roll(odd, WIDE - DR, 1)) * score_scale
        kf[cols, pl.ds(0, DL)] = total[:, :DL] + value
        kf[cols, pl.ds(DL, LANES)] = total[:, DL:]

    wing_ref[...] = kf[pl.ds(cp, lead), pl.ds(0, DK)].astype(BF16)
    own_ref[...] = kf[pl.ds(cp + lead, tok), pl.ds(0, DK)]
    pack[...] = jnp.zeros_like(pack)

    def pack_one(o, c):
        for j in range(PIECES):
            pack[o, pl.ds(j * cl, cl), :] = kf[
                pl.ds(pl.multiple_of(o * SLOT, SLOT), cl), pl.ds(j * LANES, LANES)
            ]
        return c

    lax.fori_loop(0, n, pack_one, 0)
    cg_ref[...] = pack[...].astype(BF16)


def scatter_kernel(
    n, groups, hop, tok, cl, owners,
    cg_ref, wing_ref, own_ref, lat_ref, cw_ref,
    lg_ref, wg_ref,
    crecv_buf, wrecv_buf, tot, cgrad, part, precv, pout,
    csend, crecv, wsend, wrecv, psend, precv_sem, osend, orecv,
):
    seq = lax.axis_index("seq")
    grp = lax.axis_index("grp")
    count = n * groups
    me = grp * n + seq
    per = CS // owners * SLOT
    barrier = pltpu.get_barrier_semaphore()

    def where(peer):
        return (peer // n, peer % n)

    def greet(k, c):
        pl.semaphore_signal(
            barrier, inc=1, device_id=where((me + k) % count), device_id_type=MESH
        )
        return c

    lax.fori_loop(1, count, greet, 0)
    pl.semaphore_wait(barrier, count - 1)

    def comp_copy(peer):
        return pltpu.make_async_remote_copy(
            src_ref=cg_ref.at[peer],
            dst_ref=crecv_buf.at[seq],
            send_sem=csend.at[peer],
            recv_sem=crecv.at[seq],
            device_id=(grp, peer),
            device_id_type=MESH,
        )

    def comp_arrival(peer):
        return pltpu.make_async_remote_copy(
            src_ref=cg_ref.at[peer],
            dst_ref=crecv_buf.at[peer],
            send_sem=csend.at[peer],
            recv_sem=crecv.at[peer],
            device_id=(grp, peer),
            device_id_type=MESH,
        )

    def win_copy(d):
        rows = pl.ds((hop - d) * tok, tok)
        return pltpu.make_async_remote_copy(
            src_ref=wing_ref.at[rows],
            dst_ref=wrecv_buf.at[rows],
            send_sem=wsend.at[d],
            recv_sem=wrecv.at[d],
            device_id=(grp, (seq + n - d) % n),
            device_id_type=MESH,
        )

    def part_copy(peer):
        return pltpu.make_async_remote_copy(
            src_ref=part.at[pl.ds(peer * per, per)],
            dst_ref=precv.at[me],
            send_sem=psend.at[peer],
            recv_sem=precv_sem.at[me],
            device_id=where(peer),
            device_id_type=MESH,
        )

    def part_arrival(peer):
        return pltpu.make_async_remote_copy(
            src_ref=part.at[pl.ds(0, per)],
            dst_ref=precv.at[peer],
            send_sem=psend.at[0],
            recv_sem=precv_sem.at[peer],
            device_id=where(peer),
            device_id_type=MESH,
        )

    def out_copy(peer):
        return pltpu.make_async_remote_copy(
            src_ref=pout.at[pl.ds(me * per, per)],
            dst_ref=pout.at[pl.ds(me * per, per)],
            send_sem=osend.at[peer],
            recv_sem=orecv.at[me],
            device_id=where(peer),
            device_id_type=MESH,
        )

    def out_arrival(peer):
        rows = pl.ds(peer * per, per)
        return pltpu.make_async_remote_copy(
            src_ref=pout.at[rows],
            dst_ref=pout.at[rows],
            send_sem=osend.at[peer],
            recv_sem=orecv.at[peer],
            device_id=where(peer),
            device_id_type=MESH,
        )

    def each(size, base, work):
        def one(k, c):
            work((base + k) % size)
            return c

        lax.fori_loop(1, size, one, 0)

    def to_owners(work):
        def one(peer):
            if owners == count:
                work(peer)
            else:
                pl.when(peer < owners)(lambda: work(peer))

        each(count, me, one)

    def if_owner(work):
        if owners == count:
            work()
        else:
            pl.when(me < owners)(work)

    each(n, seq, lambda peer: comp_copy(peer).start())
    for d in range(1, hop + 1):
        pl.when(seq >= d)(lambda d=d: win_copy(d).start())
    crecv_buf[seq] = cg_ref[seq]
    part[...] = jnp.zeros_like(part)
    each(n, seq, lambda peer: comp_arrival(peer).wait_recv())

    tot[...] = jnp.sum(crecv_buf[...].astype(F32), axis=0)
    for j in range(PIECES):
        cgrad[pl.ds(0, cl), pl.ds(j * LANES, LANES)] = tot[pl.ds(j * cl, cl), :]
    weight = jnp.zeros((CS, DK), F32)
    for b in range(cl):
        weight = weight + cgrad[pl.ds(b, 1), pl.ds(0, DK)] * lat_ref[pl.ds(b * CS, CS), :].astype(F32)
    for j in range(PIECES):
        w = piece_width(j)
        part[pl.ds(j, CS, stride=SLOT), pl.ds(0, w)] = weight[:, j * LANES : j * LANES + w]
    to_owners(lambda peer: part_copy(peer).start())

    for d in range(1, hop + 1):

        @pl.when(seq + d >= n)
        def _(d=d):
            wrecv_buf[pl.ds((hop - d) * tok, tok), :] = jnp.zeros((tok, DK), BF16)

    for b in range(cl):
        rows = pl.ds(b * CS, CS)
        lg_ref[rows, :] = own_ref[rows, :] + cw_ref[...] * cgrad[pl.ds(b, 1), pl.ds(0, DK)]

    @if_owner
    def _():
        precv[me] = part[pl.ds(pl.multiple_of(me * per, per), per), :]
        each(count, me, lambda peer: part_arrival(peer).wait_recv())
        pout[pl.ds(pl.multiple_of(me * per, per), per), :] = jnp.sum(precv[...], axis=0)
        each(count, me, lambda peer: out_copy(peer).start())

    for d in range(1, hop + 1):
        pl.when(seq + d < n)(lambda d=d: win_copy(d).wait_recv())
    far = lg_ref[...]
    for d in range(1, hop + 1):
        far = far + wrecv_buf[pl.ds((hop - d) * tok, tok), :].astype(F32)
    lg_ref[...] = far

    to_owners(lambda peer: out_arrival(peer).wait_recv())
    for j in range(PIECES):
        w = piece_width(j)
        wg_ref[:, pl.ds(j * LANES, w)] = pout[pl.ds(j, CS, stride=SLOT), :][:, :w]

    each(n, seq, lambda peer: comp_copy(peer).wait_send())
    for d in range(1, hop + 1):
        pl.when(seq >= d)(lambda d=d: win_copy(d).wait_send())
    to_owners(lambda peer: part_copy(peer).wait_send())
    if_owner(lambda: each(count, me, lambda peer: out_copy(peer).wait_send()))


def vmem(count):
    return [pl.BlockSpec(memory_space=pltpu.VMEM)] * count


def body(n, groups, queries, latents, cotangent, comp_weight, sel_idx, sel_count):
    tok = latents.shape[1]
    hop = (WIN + tok - 1) // tok
    lead = hop * tok
    cl = tok // CS
    pr = round_up(cl * PIECES, 16)
    cp = round_up(n * SLOT, LANES)
    nk = cp + round_up(lead + tok, LANES)
    count = n * groups
    owners = min(CS, count)
    per = CS // owners * SLOT
    own = latents[0]
    dma = pltpu.SemaphoreType.DMA

    win, comp = pl.pallas_call(
        functools.partial(gather_kernel, n, hop, tok, cl),
        out_shape=(
            jax.ShapeDtypeStruct((lead, DK), BF16),
            jax.ShapeDtypeStruct((n, pr, LANES), BF16),
        ),
        in_specs=vmem(2),
        out_specs=tuple(vmem(2)),
        scratch_shapes=[
            pltpu.VMEM((pr, LANES), F32),
            dma((hop + 1,)),
            dma((hop + 1,)),
            dma((n,)),
            dma((n,)),
        ],
        compiler_params=pltpu.CompilerParams(collective_id=0, has_side_effects=True),
    )(own, comp_weight)

    att, qg, wing, own_grad, cg = pl.pallas_call(
        functools.partial(attend_kernel, n, hop, tok, cl),
        out_shape=(
            jax.ShapeDtypeStruct((tok, H * DL), BF16),
            jax.ShapeDtypeStruct((tok, H * DK), BF16),
            jax.ShapeDtypeStruct((lead, DK), BF16),
            jax.ShapeDtypeStruct((tok, DK), F32),
            jax.ShapeDtypeStruct((n, pr, LANES), BF16),
        ),
        in_specs=vmem(6) + [pl.BlockSpec(memory_space=pltpu.SMEM)],
        out_specs=tuple(vmem(5)),
        scratch_shapes=[
            pltpu.VMEM((2, nk, WIDE), BF16),
            pltpu.VMEM((nk, WIDE), F32),
            pltpu.VMEM((H * tok, WIDE), BF16),
            pltpu.VMEM((H * tok, DL), BF16),
            pltpu.VMEM((tok, nk), F32),
            pltpu.VMEM((H * tok, nk), BF16),
            pltpu.VMEM((H * tok, nk), BF16),
            pltpu.VMEM((H * tok, WIDE), F32),
            pltpu.VMEM((n, pr, LANES), F32),
        ],
        compiler_params=pltpu.CompilerParams(vmem_limit_bytes=56 * 2**20),
    )(queries[0], cotangent[0], own, win, comp, sel_idx[0], sel_count)

    lat_grad, weight_grad = pl.pallas_call(
        functools.partial(scatter_kernel, n, groups, hop, tok, cl, owners),
        out_shape=(
            jax.ShapeDtypeStruct((tok, DK), F32),
            jax.ShapeDtypeStruct((CS, DK), F32),
        ),
        in_specs=vmem(5),
        out_specs=tuple(vmem(2)),
        scratch_shapes=[
            pltpu.VMEM((n, pr, LANES), BF16),
            pltpu.VMEM((lead, DK), BF16),
            pltpu.VMEM((pr, LANES), F32),
            pltpu.VMEM((SLOT, WIDE), F32),
            pltpu.VMEM((CS * SLOT, LANES), F32),
            pltpu.VMEM((count, per, LANES), F32),
            pltpu.VMEM((CS * SLOT, LANES), F32),
            dma((n,)),
            dma((n,)),
            dma((hop + 1,)),
            dma((hop + 1,)),
            dma((count,)),
            dma((count,)),
            dma((count,)),
            dma((count,)),
        ],
        compiler_params=pltpu.CompilerParams(collective_id=1, has_side_effects=True),
    )(cg, wing, own_grad, own, comp_weight)
    return (att[None], qg[None], lat_grad[None], weight_grad)


def solution(mesh):
    in_specs = (
        P("grp", "seq", None),
        P("grp", "seq", None),
        P("grp", "seq", None),
        P(),
        P("grp", "seq", None),
        P("grp", "seq"),
    )
    out_specs = (P("grp", "seq", None), P("grp", "seq", None), P("grp", "seq", None), P())
    return jax.shard_map(
        functools.partial(body, mesh.shape["seq"], mesh.shape["grp"]),
        mesh=mesh,
        in_specs=in_specs,
        out_specs=out_specs,
        check_vma=False,
    )
```

```python
import functools

import jax
import jax.numpy as jnp
from jax import lax
from jax.experimental import pallas as pl
from jax.experimental.pallas import tpu as pltpu
from jax.sharding import PartitionSpec as P

DL = 512
DR = 64
H = 8
QB = 64
CS = 32
WIN = 512
DK = 576
LANES = 128
WIDE = 640
PIECES = WIDE // LANES
SLOT = 8
MASKED = -1e30

MESH = pl.DeviceIdType.MESH
BF16 = jnp.bfloat16
F32 = jnp.float32
score_scale = 192.0 ** (-0.5)


def round_up(value, step):
    return (value + step - 1) // step * step


def dot_nn(a, b):
    return lax.dot_general(a, b, (((1,), (0,)), ((), ())), preferred_element_type=F32)


def dot_nt(a, b):
    return lax.dot_general(a, b, (((1,), (1,)), ((), ())), preferred_element_type=F32)


def dot_tn(a, b):
    return lax.dot_general(a, b, (((0,), (0,)), ((), ())), preferred_element_type=F32)


def piece_width(j):
    return min(LANES, DK - j * LANES)


def each(size, base, work):
    def one(k, c):
        work((base + k) % size)
        return c

    lax.fori_loop(1, size, one, 0)


def kernel(
    n, groups, hop, tok, cl, owners,
    q_ref, cot_ref, lat_ref, cw_ref, idx_ref, cnt_ref,
    att_ref, qg_ref, lg_ref, wg_ref,
    qq, cc, win, comp, tmp, kk, kf, bias, ds_ref, pp, dq, att_buf, qg_buf,
    pack, cg, crecv_buf, cgrad, part, precv, pout, wing, srecv, wrecv,
    load_sem, save_sem,
    gc_send, gc_recv, gw_send, gw_recv, gs_send, gs_recv,
    rc_send, rc_recv, rs_send, rs_recv, rw_send, rw_recv,
    p_send, p_recv, o_send, o_recv,
):
    seq = lax.axis_index("seq")
    grp = lax.axis_index("grp")
    count = n * groups
    me = grp * n + seq
    parity = seq % 2
    base = seq - parity
    sibling = base + 1 - parity
    per = CS // owners * SLOT
    nk = bias.shape[1]
    lead = hop * tok
    ext = lead + tok
    cp = nk - round_up(ext, LANES)
    half = (H // 2) * tok
    pair = 2 * DK
    reach = hop // 2

    def where(peer):
        return (peer // n, peer % n)

    def remote(src, dst, send, recv, device):
        return pltpu.make_async_remote_copy(
            src_ref=src, dst_ref=dst, send_sem=send, recv_sem=recv,
            device_id=device, device_id_type=MESH,
        )

    def segment(d):
        return pl.ds((hop - d) * tok, tok)

    barrier = pltpu.get_barrier_semaphore()
    each(
        count, me,
        lambda peer: pl.semaphore_signal(
            barrier, inc=1, device_id=where(peer), device_id_type=MESH
        ),
    )

    loads = []
    for m in range(H // 2):
        for p in range(2):
            rows = pl.ds(p * half + m * tok, tok)
            at = 2 * (2 * m + p)
            loads.append(
                pltpu.make_async_copy(
                    q_ref.at[:, pl.ds(m * pair + p * DL, WIDE)], qq.at[rows], load_sem.at[at]
                )
            )
            loads.append(
                pltpu.make_async_copy(
                    cot_ref.at[:, pl.ds((2 * m + p) * DL, DL)], cc.at[rows], load_sem.at[at + 1]
                )
            )
    for load in loads:
        load.start()

    tmp[...] = jnp.zeros_like(tmp)
    for b in range(cl):
        block = lat_ref[pl.ds(b * CS, CS), :].astype(F32) * cw_ref[...]
        row = jnp.sum(block, axis=0, keepdims=True)
        for j in range(PIECES):
            w = piece_width(j)
            tmp[pl.ds(j * cl + b, 1), pl.ds(0, w)] = row[:, j * LANES : j * LANES + w]
    comp[seq] = tmp[...].astype(BF16)
    pl.semaphore_wait(barrier, count - 1)

    def comp_send(peer):
        return remote(comp.at[seq], comp.at[seq], gc_send.at[peer], gc_recv.at[seq], (grp, peer))

    def comp_wait(peer):
        return remote(comp.at[peer], comp.at[peer], gc_send.at[peer], gc_recv.at[peer], (grp, peer))

    def win_copy(k):
        return remote(
            lat_ref, win.at[segment(2 * k)], gw_send.at[k], gw_recv.at[k],
            (grp, (seq + 2 * k) % n),
        )

    def pass_on(k, d):
        src = lat_ref if k == 0 else win.at[segment(2 * k)]
        return remote(src, win.at[segment(d)], gs_send.at[k], gs_recv.at[d], (grp, sibling))

    def forwarded(work):
        for k in range(reach + 1):
            if k < reach:
                pl.when((parity == 0) & (base >= 2 * k))(lambda k=k: work(k, 2 * k + 1, True))
            if k > 0:
                pl.when((parity == 1) & (base >= 2 * k))(lambda k=k: work(k, 2 * k - 1, False))

    for k in range(reach, 0, -1):
        pl.when(base + 2 * k < n)(lambda k=k: win_copy(k).start())
    pl.when(parity == 0)(lambda: pass_on(0, 1).start())
    each(n, seq, lambda peer: comp_send(peer).start())

    for d in range(1, hop + 1):

        @pl.when(seq < d)
        def _(d=d):
            win[segment(d), :] = jnp.zeros((tok, DK), BF16)

    blocks = tok // QB
    slots = idx_ref.shape[1]
    key_id = lax.broadcasted_iota(jnp.int32, (cp, slots), 0)
    in_slot = key_id % SLOT
    comp_id = jnp.where(in_slot < cl, (key_id // SLOT) * cl + in_slot, -1)
    slot_id = lax.broadcasted_iota(jnp.int32, (cp, slots), 1)
    for r in range(blocks):
        chosen = idx_ref[pl.ds(r, 1), :]
        hit = (comp_id == chosen) & (slot_id < cnt_ref[0, r])
        hit = jnp.where(hit, 1.0, 0.0).astype(BF16)
        live = dot_nt(jnp.ones((QB, slots), BF16), hit)
        bias[pl.ds(r * QB, QB), pl.ds(0, cp)] = jnp.where(live > 0.5, 0.0, MASKED)
    wide = nk - cp
    row = lax.broadcasted_iota(jnp.int32, (tok, wide), 0)
    col = lax.broadcasted_iota(jnp.int32, (tok, wide), 1)
    shift = lead - WIN
    ok = (col > row + shift) & (col <= row + lead) & (col - lead + seq * tok >= 0)
    bias[:, pl.ds(cp, wide)] = jnp.where(ok, 0.0, MASKED)
    kf[pl.ds(0, cp), :] = jnp.zeros((cp, WIDE), F32)
    kf[pl.ds(cp, ext), pl.ds(DL, LANES)] = jnp.zeros((ext, LANES), F32)
    kf[pl.ds(cp + lead, tok), pl.ds(0, DK)] = lat_ref[...].astype(F32)
    if nk > cp + ext:
        kf[pl.ds(cp + ext, nk - cp - ext), :] = jnp.zeros((nk - cp - ext, WIDE), F32)
    pack[...] = jnp.zeros_like(pack)
    part[...] = jnp.zeros_like(part)

    for k in range(1, reach + 1):

        @pl.when(base >= 2 * k)
        def _(k=k):
            win_copy(k).wait_recv()
            if k < reach:
                pl.when(parity == 0)(lambda: pass_on(k, 2 * k + 1).start())
            pl.when(parity == 1)(lambda: pass_on(k, 2 * k - 1).start())

    each(n, seq, lambda peer: comp_wait(peer).wait_recv())

    def unpack(o, c):
        packed = comp[o].astype(F32)
        for j in range(PIECES):
            kf[pl.ds(pl.multiple_of(o * SLOT, SLOT), cl), pl.ds(j * LANES, LANES)] = packed[
                j * cl : (j + 1) * cl, :
            ]
        return c

    lax.fori_loop(0, n, unpack, 0)

    def sibling_arrival(k, d):
        pass_on(k, d).wait_recv()

    for k in range(reach + 1):
        if k < reach:
            pl.when((parity == 1) & (base >= 2 * k))(lambda k=k: sibling_arrival(k, 2 * k + 1))
        if k > 0:
            pl.when((parity == 0) & (base >= 2 * k))(lambda k=k: sibling_arrival(k, 2 * k - 1))
    kf[pl.ds(cp, lead), pl.ds(0, DK)] = win[...].astype(F32)
    kk[0] = kf[...].astype(BF16)
    kk[1] = pltpu.roll(kf[...], DR, 1).astype(BF16)
    for load in loads:
        load.wait()

    step = min(256, half)
    heads = step // tok
    for c in range(2 * half // step):
        p = c * step // half
        rows = pl.ds(c * step, step)
        keys = kk[p]
        values = kk[0, :, pl.ds(0, DL)]
        s = dot_nt(qq[rows, :], keys) * score_scale
        s = (s.reshape(heads, tok, nk) + bias[...][None]).reshape(step, nk)
        e = jnp.exp(s - jnp.max(s, axis=1, keepdims=True))
        w = e * (1.0 / jnp.sum(e, axis=1, keepdims=True))
        rounded = w.astype(BF16)
        pp[rows, :] = rounded
        context = dot_nn(rounded, values)
        grads = cc[rows, :]
        row_dot = jnp.sum(grads.astype(F32) * context, axis=1, keepdims=True)
        dscore = (w * (dot_nt(grads, values) - row_dot)).astype(BF16)
        ds_ref[rows, :] = dscore
        dq[rows, :] = dot_nn(dscore, keys) * score_scale
        for i in range(heads):
            m = (c * step - p * half) // tok + i
            att_buf[:, pl.ds((2 * m + p) * DL, DL)] = context[i * tok : (i + 1) * tok].astype(BF16)

    save_att = pltpu.make_async_copy(att_buf, att_ref, save_sem.at[0])
    save_att.start()

    def key_pass(start):
        size = min(256, nk - start)
        cols = pl.ds(start, size)
        even = dot_tn(ds_ref[pl.ds(0, half), cols], qq[pl.ds(0, half), :])
        odd = dot_tn(ds_ref[pl.ds(half, half), cols], qq[pl.ds(half, half), :])
        value = dot_tn(pp[:, cols], cc[...])
        total = (even + pltpu.roll(odd, WIDE - DR, 1)) * score_scale
        kf[cols, pl.ds(0, DL)] = total[:, :DL] + value
        kf[cols, pl.ds(DL, LANES)] = total[:, DL:]

    def seg_grad(d):
        return kf[pl.ds(cp + (hop - d) * tok, tok), pl.ds(0, DK)]

    def sum_send(peer):
        return remote(cg.at[peer], crecv_buf.at[seq], rc_send.at[peer], rc_recv.at[seq], (grp, peer))

    def sum_wait(peer):
        return remote(
            cg.at[peer], crecv_buf.at[peer], rc_send.at[peer], rc_recv.at[peer], (grp, peer)
        )

    def to_sibling(k, d):
        return remote(
            wing.at[segment(d)], srecv.at[k], rs_send.at[k], rs_recv.at[k], (grp, sibling)
        )

    def to_source(k):
        return remote(
            wing.at[segment(2 * k)], wrecv.at[k - 1], rw_send.at[k], rw_recv.at[k],
            (grp, (seq + n - 2 * k) % n),
        )

    def part_copy(peer):
        return remote(
            part.at[pl.ds(peer * per, per)], precv.at[me], p_send.at[peer], p_recv.at[me],
            where(peer),
        )

    def part_wait(peer):
        return remote(
            part.at[pl.ds(0, per)], precv.at[peer], p_send.at[0], p_recv.at[peer], where(peer)
        )

    def out_copy(peer):
        rows = pl.ds(me * per, per)
        return remote(pout.at[rows], pout.at[rows], o_send.at[peer], o_recv.at[me], where(peer))

    def out_wait(peer):
        rows = pl.ds(peer * per, per)
        return remote(pout.at[rows], pout.at[rows], o_send.at[peer], o_recv.at[peer], where(peer))

    def to_owners(work):
        def one(peer):
            if owners == count:
                work(peer)
            else:
                pl.when(peer < owners)(lambda: work(peer))

        each(count, me, one)

    def if_owner(work):
        if owners == count:
            work()
        else:
            pl.when(me < owners)(work)

    done = 0
    while done < cp:
        key_pass(done)
        done += 256

    def pack_one(o, c):
        for j in range(PIECES):
            pack[o, pl.ds(j * cl, cl), :] = kf[
                pl.ds(pl.multiple_of(o * SLOT, SLOT), cl), pl.ds(j * LANES, LANES)
            ]
        return c

    lax.fori_loop(0, n, pack_one, 0)
    cg[...] = pack[...].astype(BF16)
    crecv_buf[seq] = cg[seq]
    each(n, seq, lambda peer: sum_send(peer).start())

    while done < nk:
        key_pass(done)
        done += 256

    def send_sibling(k, d, unused):
        wing[segment(d), :] = seg_grad(d).astype(BF16)
        to_sibling(k, d).start()

    def back(work):
        for k in range(reach, -1, -1):
            if k > 0:
                pl.when((parity == 0) & (base >= 2 * k))(lambda k=k: work(k, 2 * k - 1, True))
            if k < reach:
                pl.when((parity == 1) & (base >= 2 * k))(lambda k=k: work(k, 2 * k + 1, False))

    back(send_sibling)

    @pl.when((parity == 0) & (base >= hop))
    def _():
        wing[segment(hop), :] = seg_grad(hop).astype(BF16)
        to_source(reach).start()

    each(n, seq, lambda peer: sum_wait(peer).wait_recv())
    total = jnp.sum(crecv_buf[...].astype(F32), axis=0)
    for j in range(PIECES):
        cgrad[pl.ds(0, cl), pl.ds(j * LANES, LANES)] = total[j * cl : (j + 1) * cl, :]
    weight = jnp.zeros((CS, DK), F32)
    for b in range(cl):
        weight = weight + cgrad[pl.ds(b, 1), pl.ds(0, DK)] * lat_ref[pl.ds(b * CS, CS), :].astype(F32)
    for j in range(PIECES):
        w = piece_width(j)
        part[pl.ds(j, CS, stride=SLOT), pl.ds(0, w)] = weight[:, j * LANES : j * LANES + w]
    to_owners(lambda peer: part_copy(peer).start())

    def merge(k):
        to_sibling(k, 1).wait_recv()
        wing[segment(2 * k), :] = (seg_grad(2 * k) + srecv[k].astype(F32)).astype(BF16)
        to_source(k).start()

    for k in range(reach, 0, -1):
        if k < reach:
            pl.when(base >= 2 * k)(lambda k=k: merge(k))
        else:
            pl.when((parity == 1) & (base >= 2 * k))(lambda k=k: merge(k))

    @if_owner
    def _():
        precv[me] = part[pl.ds(pl.multiple_of(me * per, per), per), :]
        each(count, me, lambda peer: part_wait(peer).wait_recv())
        pout[pl.ds(pl.multiple_of(me * per, per), per), :] = jnp.sum(precv[...], axis=0)
        each(count, me, lambda peer: out_copy(peer).start())

    for m in range(H // 2):
        even = pl.ds(m * tok, tok)
        odd = pl.ds(half + m * tok, tok)
        qg_buf[:, pl.ds(m * pair, DL)] = dq[even, pl.ds(0, DL)].astype(BF16)
        qg_buf[:, pl.ds(m * pair + DL, LANES)] = (
            dq[even, pl.ds(DL, LANES)] + dq[odd, pl.ds(0, LANES)]
        ).astype(BF16)
        qg_buf[:, pl.ds(m * pair + WIDE, DL)] = dq[odd, pl.ds(LANES, DL)].astype(BF16)
    save_qg = pltpu.make_async_copy(qg_buf, qg_ref, save_sem.at[1])
    save_qg.start()

    own = seg_grad(0)
    for b in range(cl):
        rows = pl.ds(b * CS, CS)
        lg_ref[rows, :] = own[b * CS : (b + 1) * CS] + cw_ref[...] * cgrad[pl.ds(b, 1), pl.ds(0, DK)]

    @pl.when(parity == 0)
    def _():
        to_sibling(0, 1).wait_recv()
        lg_ref[...] += srecv[0].astype(F32)

    for k in range(1, reach + 1):

        @pl.when(base + 2 * k < n)
        def _(k=k):
            to_source(k).wait_recv()
            lg_ref[...] += wrecv[k - 1].astype(F32)

    to_owners(lambda peer: out_wait(peer).wait_recv())
    for j in range(PIECES):
        w = piece_width(j)
        wg_ref[:, pl.ds(j * LANES, w)] = pout[pl.ds(j, CS, stride=SLOT), :][:, :w]

    save_att.wait()
    save_qg.wait()
    each(n, seq, lambda peer: comp_send(peer).wait_send())
    each(n, seq, lambda peer: sum_send(peer).wait_send())
    for k in range(1, reach + 1):
        pl.when(base + 2 * k < n)(lambda k=k: win_copy(k).wait_send())
        pl.when(base >= 2 * k)(lambda k=k: to_source(k).wait_send())
    forwarded(lambda k, d, unused: pass_on(k, d).wait_send())
    back(lambda k, d, unused: to_sibling(k, d).wait_send())
    to_owners(lambda peer: part_copy(peer).wait_send())
    if_owner(lambda: each(count, me, lambda peer: out_copy(peer).wait_send()))


def body(n, groups, queries, latents, cotangent, comp_weight, sel_idx, sel_count):
    tok = latents.shape[1]
    hop = (WIN + tok - 1) // tok
    assert hop % 2 == 0 and n % 2 == 0
    lead = hop * tok
    cl = tok // CS
    pr = round_up(cl * PIECES, 16)
    nk = round_up(n * SLOT, LANES) + round_up(lead + tok, LANES)
    count = n * groups
    owners = min(CS, count)
    per = CS // owners * SLOT
    dma = pltpu.SemaphoreType.DMA
    reach = hop // 2
    any_spec = pl.BlockSpec(memory_space=pl.ANY)
    vmem_spec = pl.BlockSpec(memory_space=pltpu.VMEM)
    att, qg, lat_grad, weight_grad = pl.pallas_call(
        functools.partial(kernel, n, groups, hop, tok, cl, owners),
        out_shape=(
            jax.ShapeDtypeStruct((tok, H * DL), BF16),
            jax.ShapeDtypeStruct((tok, H * DK), BF16),
            jax.ShapeDtypeStruct((tok, DK), F32),
            jax.ShapeDtypeStruct((CS, DK), F32),
        ),
        in_specs=[
            any_spec,
            any_spec,
            vmem_spec,
            vmem_spec,
            vmem_spec,
            pl.BlockSpec(memory_space=pltpu.SMEM),
        ],
        out_specs=(any_spec, any_spec, vmem_spec, vmem_spec),
        scratch_shapes=[
            pltpu.VMEM((H * tok, WIDE), BF16),
            pltpu.VMEM((H * tok, DL), BF16),
            pltpu.VMEM((lead, DK), BF16),
            pltpu.VMEM((n, pr, LANES), BF16),
            pltpu.VMEM((pr, LANES), F32),
            pltpu.VMEM((2, nk, WIDE), BF16),
            pltpu.VMEM((nk, WIDE), F32),
            pltpu.VMEM((tok, nk), F32),
            pltpu.VMEM((H * tok, nk), BF16),
            pltpu.VMEM((H * tok, nk), BF16),
            pltpu.VMEM((H * tok, WIDE), F32),
            pltpu.VMEM((tok, H * DL), BF16),
            pltpu.VMEM((tok, H * DK), BF16),
            pltpu.VMEM((n, pr, LANES), F32),
            pltpu.VMEM((n, pr, LANES), BF16),
            pltpu.VMEM((n, pr, LANES), BF16),
            pltpu.VMEM((SLOT, WIDE), F32),
            pltpu.VMEM((CS * SLOT, LANES), F32),
            pltpu.VMEM((count, per, LANES), F32),
            pltpu.VMEM((CS * SLOT, LANES), F32),
            pltpu.VMEM((lead, DK), BF16),
            pltpu.VMEM((reach + 1, tok, DK), BF16),
            pltpu.VMEM((reach, tok, DK), BF16),
            dma((2 * H,)),
            dma((2,)),
            dma((n,)),
            dma((n,)),
            dma((reach + 1,)),
            dma((reach + 1,)),
            dma((reach + 1,)),
            dma((hop + 1,)),
            dma((n,)),
            dma((n,)),
            dma((reach + 1,)),
            dma((reach + 1,)),
            dma((reach + 1,)),
            dma((reach + 1,)),
            dma((count,)),
            dma((count,)),
            dma((count,)),
            dma((count,)),
        ],
        compiler_params=pltpu.CompilerParams(
            collective_id=0, has_side_effects=True, vmem_limit_bytes=56 * 2**20
        ),
    )(queries[0], cotangent[0], latents[0], comp_weight, sel_idx[0], sel_count)
    return (att[None], qg[None], lat_grad[None], weight_grad)


def solution(mesh):
    in_specs = (
        P("grp", "seq", None),
        P("grp", "seq", None),
        P("grp", "seq", None),
        P(),
        P("grp", "seq", None),
        P("grp", "seq"),
    )
    out_specs = (P("grp", "seq", None), P("grp", "seq", None), P("grp", "seq", None), P())
    return jax.shard_map(
        functools.partial(body, mesh.shape["seq"], mesh.shape["grp"]),
        mesh=mesh,
        in_specs=in_specs,
        out_specs=out_specs,
        check_vma=False,
    )
```

```python
import functools

import jax
import jax.numpy as jnp
from jax import lax
from jax.experimental import pallas as pl
from jax.experimental.pallas import tpu as pltpu
from jax.sharding import PartitionSpec as P

DL = 512
DR = 64
H = 8
QB = 64
CS = 32
WIN = 512
DK = 576
LANES = 128
WIDE = 640
PIECES = WIDE // LANES
SLOT = 8
MASKED = -1e30
UNROLL = 32

MESH = pl.DeviceIdType.MESH
BF16 = jnp.bfloat16
F32 = jnp.float32
score_scale = 192.0 ** (-0.5)


def round_up(value, step):
    return (value + step - 1) // step * step


def dot_nn(a, b):
    return lax.dot_general(a, b, (((1,), (0,)), ((), ())), preferred_element_type=F32)


def dot_nt(a, b):
    return lax.dot_general(a, b, (((1,), (1,)), ((), ())), preferred_element_type=F32)


def dot_tn(a, b):
    return lax.dot_general(a, b, (((0,), (0,)), ((), ())), preferred_element_type=F32)


def piece_width(j):
    return min(LANES, DK - j * LANES)


def each(size, base, work):
    if size <= UNROLL:
        for k in range(1, size):
            work(lax.rem(base + k, size))
        return

    def one(k, c):
        work(lax.rem(base + k, size))
        return c

    lax.fori_loop(1, size, one, 0)


def kernel(
    n, groups, hop, tok, cl, owners,
    q_ref, cot_ref, lat_t_ref, cw_ref, idx_ref, cnt_ref,
    att_ref, qg_ref, lg_t_ref, wg_ref,
    lat_ref, lg_ref, qq, cc, win, comp, tmp, kk, kf, bias, ds_ref, pp, dq, att_buf, qg_buf,
    pack, cg, crecv_buf, cgrad, part, precv, pout, wing, srecv, wrecv,
    load_sem, save_sem,
    gc_send, gc_recv, gw_send, gw_recv, gs_send, gs_recv,
    rc_send, rc_recv, rs_send, rs_recv, rw_send, rw_recv,
    p_send, p_recv, o_send, o_recv,
):
    seq = lax.axis_index("seq")
    grp = lax.axis_index("grp")
    count = n * groups
    me = grp * n + seq
    parity = seq % 2
    base = seq - parity
    sibling = base + 1 - parity
    per = CS // owners * SLOT
    nk = bias.shape[1]
    lead = hop * tok
    ext = lead + tok
    cp = nk - round_up(ext, LANES)
    half = (H // 2) * tok
    pair = 2 * DK
    reach = hop // 2

    def where(peer):
        return (lax.div(peer, n), lax.rem(peer, n))

    def remote(src, dst, send, recv, device):
        return pltpu.make_async_remote_copy(
            src_ref=src, dst_ref=dst, send_sem=send, recv_sem=recv,
            device_id=device, device_id_type=MESH,
        )

    def wait_all(ref, sem):
        remote(ref, ref, sem, sem, (grp, sibling)).wait_recv()

    def segment(d):
        return pl.ds((hop - d) * tok, tok)

    barrier = pltpu.get_barrier_semaphore()
    each(
        count, me,
        lambda peer: pl.semaphore_signal(
            barrier, inc=1, device_id=where(peer), device_id_type=MESH
        ),
    )

    loads = []
    for m in range(H // 2):
        for p in range(2):
            rows = pl.ds(p * half + m * tok, tok)
            at = 2 * (2 * m + p)
            loads.append(
                pltpu.make_async_copy(
                    q_ref.at[:, pl.ds(m * pair + p * DL, WIDE)], qq.at[rows], load_sem.at[at]
                )
            )
            loads.append(
                pltpu.make_async_copy(
                    cot_ref.at[:, pl.ds((2 * m + p) * DL, DL)], cc.at[rows], load_sem.at[at + 1]
                )
            )
    for load in loads:
        load.start()

    lat_ref[...] = lat_t_ref[...].astype(F32).T.astype(BF16)
    tmp[...] = jnp.zeros_like(tmp)
    for b in range(cl):
        block = lat_ref[pl.ds(b * CS, CS), :].astype(F32) * cw_ref[...]
        row = jnp.sum(block, axis=0, keepdims=True)
        for j in range(PIECES):
            w = piece_width(j)
            tmp[pl.ds(j * cl + b, 1), pl.ds(0, w)] = row[:, j * LANES : j * LANES + w]
    comp[seq] = tmp[...].astype(BF16)
    pl.semaphore_wait(barrier, count - 1)

    def comp_send(peer):
        return remote(comp.at[seq], comp.at[seq], gc_send, gc_recv, (grp, peer))

    def win_copy(k):
        return remote(
            lat_ref, win.at[segment(2 * k)], gw_send.at[k], gw_recv.at[k],
            (grp, (seq + 2 * k) % n),
        )

    def pass_on(k, d):
        src = lat_ref if k == 0 else win.at[segment(2 * k)]
        return remote(src, win.at[segment(d)], gs_send.at[k], gs_recv.at[d], (grp, sibling))

    def forwarded(work):
        for k in range(reach + 1):
            if k < reach:
                pl.when((parity == 0) & (base >= 2 * k))(lambda k=k: work(k, 2 * k + 1, True))
            if k > 0:
                pl.when((parity == 1) & (base >= 2 * k))(lambda k=k: work(k, 2 * k - 1, False))

    for k in range(reach, 0, -1):
        pl.when(base + 2 * k < n)(lambda k=k: win_copy(k).start())
    pl.when(parity == 0)(lambda: pass_on(0, 1).start())
    each(n, seq, lambda peer: comp_send(peer).start())

    for d in range(1, hop + 1):

        @pl.when(seq < d)
        def _(d=d):
            win[segment(d), :] = jnp.zeros((tok, DK), BF16)

    blocks = tok // QB
    slots = idx_ref.shape[1]
    key_id = lax.broadcasted_iota(jnp.int32, (cp, slots), 0)
    in_slot = key_id % SLOT
    comp_id = jnp.where(in_slot < cl, (key_id // SLOT) * cl + in_slot, -1)
    slot_id = lax.broadcasted_iota(jnp.int32, (cp, slots), 1)
    for r in range(blocks):
        chosen = idx_ref[pl.ds(r, 1), :]
        hit = (comp_id == chosen) & (slot_id < cnt_ref[0, r])
        hit = jnp.where(hit, 1.0, 0.0).astype(BF16)
        live = dot_nt(jnp.ones((QB, slots), BF16), hit)
        bias[pl.ds(r * QB, QB), pl.ds(0, cp)] = jnp.where(live > 0.5, 0.0, MASKED)
    wide = nk - cp
    row = lax.broadcasted_iota(jnp.int32, (tok, wide), 0)
    col = lax.broadcasted_iota(jnp.int32, (tok, wide), 1)
    shift = lead - WIN
    ok = (col > row + shift) & (col <= row + lead) & (col - lead + seq * tok >= 0)
    bias[:, pl.ds(cp, wide)] = jnp.where(ok, 0.0, MASKED)
    kf[pl.ds(0, cp), :] = jnp.zeros((cp, WIDE), F32)
    kf[pl.ds(cp, ext), pl.ds(DL, LANES)] = jnp.zeros((ext, LANES), F32)
    kf[pl.ds(cp + lead, tok), pl.ds(0, DK)] = lat_ref[...].astype(F32)
    if nk > cp + ext:
        kf[pl.ds(cp + ext, nk - cp - ext), :] = jnp.zeros((nk - cp - ext, WIDE), F32)
    pack[...] = jnp.zeros_like(pack)
    part[...] = jnp.zeros_like(part)

    for k in range(1, reach + 1):

        @pl.when(base >= 2 * k)
        def _(k=k):
            win_copy(k).wait_recv()
            if k < reach:
                pl.when(parity == 0)(lambda: pass_on(k, 2 * k + 1).start())
            pl.when(parity == 1)(lambda: pass_on(k, 2 * k - 1).start())

    wait_all(comp.at[pl.ds(0, n - 1)], gc_recv)

    def unpack(o, c):
        packed = comp[o].astype(F32)
        for j in range(PIECES):
            kf[pl.ds(pl.multiple_of(o * SLOT, SLOT), cl), pl.ds(j * LANES, LANES)] = packed[
                j * cl : (j + 1) * cl, :
            ]
        return c

    lax.fori_loop(0, n, unpack, 0)

    def sibling_arrival(k, d):
        pass_on(k, d).wait_recv()

    for k in range(reach + 1):
        if k < reach:
            pl.when((parity == 1) & (base >= 2 * k))(lambda k=k: sibling_arrival(k, 2 * k + 1))
        if k > 0:
            pl.when((parity == 0) & (base >= 2 * k))(lambda k=k: sibling_arrival(k, 2 * k - 1))
    kf[pl.ds(cp, lead), pl.ds(0, DK)] = win[...].astype(F32)
    kk[0] = kf[...].astype(BF16)
    kk[1] = pltpu.roll(kf[...], DR, 1).astype(BF16)
    for load in loads:
        load.wait()

    step = min(256, half)
    heads = step // tok
    for c in range(2 * half // step):
        p = c * step // half
        rows = pl.ds(c * step, step)
        keys = kk[p]
        values = kk[0, :, pl.ds(0, DL)]
        s = dot_nt(qq[rows, :], keys) * score_scale
        s = (s.reshape(heads, tok, nk) + bias[...][None]).reshape(step, nk)
        e = jnp.exp(s - jnp.max(s, axis=1, keepdims=True))
        w = e * (1.0 / jnp.sum(e, axis=1, keepdims=True))
        rounded = w.astype(BF16)
        pp[rows, :] = rounded
        context = dot_nn(rounded, values)
        grads = cc[rows, :]
        row_dot = jnp.sum(grads.astype(F32) * context, axis=1, keepdims=True)
        dscore = (w * (dot_nt(grads, values) - row_dot)).astype(BF16)
        ds_ref[rows, :] = dscore
        dq[rows, :] = dot_nn(dscore, keys) * score_scale
        for i in range(heads):
            m = (c * step - p * half) // tok + i
            att_buf[:, pl.ds((2 * m + p) * DL, DL)] = context[i * tok : (i + 1) * tok].astype(BF16)

    save_att = pltpu.make_async_copy(att_buf, att_ref, save_sem.at[0])
    save_att.start()

    def key_pass(start):
        size = min(256, nk - start)
        cols = pl.ds(start, size)
        even = dot_tn(ds_ref[pl.ds(0, half), cols], qq[pl.ds(0, half), :])
        odd = dot_tn(ds_ref[pl.ds(half, half), cols], qq[pl.ds(half, half), :])
        value = dot_tn(pp[:, cols], cc[...])
        total = (even + pltpu.roll(odd, WIDE - DR, 1)) * score_scale
        kf[cols, pl.ds(0, DL)] = total[:, :DL] + value
        kf[cols, pl.ds(DL, LANES)] = total[:, DL:]

    def seg_grad(d):
        return kf[pl.ds(cp + (hop - d) * tok, tok), pl.ds(0, DK)]

    def sum_send(peer):
        return remote(cg.at[peer], crecv_buf.at[seq], rc_send, rc_recv, (grp, peer))

    def to_sibling(k, d):
        return remote(
            wing.at[segment(d)], srecv.at[k], rs_send.at[k], rs_recv.at[k], (grp, sibling)
        )

    def to_source(k):
        return remote(
            wing.at[segment(2 * k)], wrecv.at[k - 1], rw_send.at[k], rw_recv.at[k],
            (grp, (seq + n - 2 * k) % n),
        )

    def part_copy(peer):
        return remote(
            part.at[pl.ds(peer * per, per)], precv.at[me], p_send, p_recv, where(peer)
        )

    def out_copy(peer):
        rows = pl.ds(me * per, per)
        return remote(pout.at[rows], pout.at[rows], o_send, o_recv, where(peer))

    def wait_owners(ref, sem):
        if owners == count:
            wait_all(ref.at[pl.ds(0, (owners - 1) * per)], sem)
        else:
            pl.when(me < owners)(lambda: wait_all(ref.at[pl.ds(0, (owners - 1) * per)], sem))
            pl.when(me >= owners)(lambda: wait_all(ref.at[pl.ds(0, owners * per)], sem))

    def to_owners(work):
        def one(peer):
            if owners == count:
                work(peer)
            else:
                pl.when(peer < owners)(lambda: work(peer))

        each(count, me, one)

    def if_owner(work):
        if owners == count:
            work()
        else:
            pl.when(me < owners)(work)

    done = 0
    while done < cp:
        key_pass(done)
        done += 256

    def pack_one(o, c):
        for j in range(PIECES):
            pack[o, pl.ds(j * cl, cl), :] = kf[
                pl.ds(pl.multiple_of(o * SLOT, SLOT), cl), pl.ds(j * LANES, LANES)
            ]
        return c

    lax.fori_loop(0, n, pack_one, 0)
    cg[...] = pack[...].astype(BF16)
    crecv_buf[seq] = cg[seq]
    each(n, seq, lambda peer: sum_send(peer).start())

    def send_sibling(k, d):
        wing[segment(d), :] = seg_grad(d).astype(BF16)
        to_sibling(k, d).start()

    def back(work):
        for k in range(reach, -1, -1):
            if k > 0:
                pl.when((parity == 0) & (base >= 2 * k))(lambda k=k: work(k, 2 * k - 1, True))
            if k < reach:
                pl.when((parity == 1) & (base >= 2 * k))(lambda k=k: work(k, 2 * k + 1, False))

    def ship(d):
        if d == hop:

            @pl.when((parity == 0) & (base >= hop))
            def _():
                wing[segment(hop), :] = seg_grad(hop).astype(BF16)
                to_source(reach).start()

        elif d % 2 == 1:
            k = (d + 1) // 2
            pl.when((parity == 0) & (base >= 2 * k))(lambda: send_sibling(k, d))
            pl.when((parity == 1) & (base >= 2 * k - 2))(lambda: send_sibling(k - 1, d))

    ready = hop
    while True:
        while ready > 0 and cp + (hop - ready + 1) * tok <= done:
            ship(ready)
            ready -= 1
        if done >= nk:
            break
        key_pass(done)
        done += 256

    wait_all(crecv_buf.at[pl.ds(0, n - 1)], rc_recv)
    total = jnp.sum(crecv_buf[...].astype(F32), axis=0)
    for j in range(PIECES):
        cgrad[pl.ds(0, cl), pl.ds(j * LANES, LANES)] = total[j * cl : (j + 1) * cl, :]
    weight = jnp.zeros((CS, DK), F32)
    for b in range(cl):
        weight = weight + cgrad[pl.ds(b, 1), pl.ds(0, DK)] * lat_ref[pl.ds(b * CS, CS), :].astype(F32)
    for j in range(PIECES):
        w = piece_width(j)
        part[pl.ds(j, CS, stride=SLOT), pl.ds(0, w)] = weight[:, j * LANES : j * LANES + w]
    to_owners(lambda peer: part_copy(peer).start())

    def merge(k):
        to_sibling(k, 1).wait_recv()
        wing[segment(2 * k), :] = (seg_grad(2 * k) + srecv[k].astype(F32)).astype(BF16)
        to_source(k).start()

    for k in range(reach, 0, -1):
        if k < reach:
            pl.when(base >= 2 * k)(lambda k=k: merge(k))
        else:
            pl.when((parity == 1) & (base >= 2 * k))(lambda k=k: merge(k))

    @if_owner
    def _():
        precv[me] = part[pl.ds(pl.multiple_of(me * per, per), per), :]
        wait_all(precv.at[pl.ds(0, count - 1)], p_recv)
        pout[pl.ds(pl.multiple_of(me * per, per), per), :] = jnp.sum(precv[...], axis=0)
        each(count, me, lambda peer: out_copy(peer).start())

    for m in range(H // 2):
        even = pl.ds(m * tok, tok)
        odd = pl.ds(half + m * tok, tok)
        qg_buf[:, pl.ds(m * pair, DL)] = dq[even, pl.ds(0, DL)].astype(BF16)
        qg_buf[:, pl.ds(m * pair + DL, LANES)] = (
            dq[even, pl.ds(DL, LANES)] + dq[odd, pl.ds(0, LANES)]
        ).astype(BF16)
        qg_buf[:, pl.ds(m * pair + WIDE, DL)] = dq[odd, pl.ds(LANES, DL)].astype(BF16)
    save_qg = pltpu.make_async_copy(qg_buf, qg_ref, save_sem.at[1])
    save_qg.start()

    own = seg_grad(0)
    for b in range(cl):
        rows = pl.ds(b * CS, CS)
        lg_ref[rows, :] = own[b * CS : (b + 1) * CS] + cw_ref[...] * cgrad[pl.ds(b, 1), pl.ds(0, DK)]

    @pl.when(parity == 0)
    def _():
        to_sibling(0, 1).wait_recv()
        lg_ref[...] += srecv[0].astype(F32)

    for k in range(1, reach + 1):

        @pl.when(base + 2 * k < n)
        def _(k=k):
            to_source(k).wait_recv()
            lg_ref[...] += wrecv[k - 1].astype(F32)

    lg_t_ref[...] = lg_ref[...].T
    wait_owners(pout, o_recv)
    for j in range(PIECES):
        w = piece_width(j)
        wg_ref[:, pl.ds(j * LANES, w)] = pout[pl.ds(j, CS, stride=SLOT), :][:, :w]

    save_att.wait()
    save_qg.wait()
    wait_all(comp.at[pl.ds(0, n - 1)], gc_send)
    wait_all(cg.at[pl.ds(0, n - 1)], rc_send)
    for k in range(1, reach + 1):
        pl.when(base + 2 * k < n)(lambda k=k: win_copy(k).wait_send())
        pl.when(base >= 2 * k)(lambda k=k: to_source(k).wait_send())
    forwarded(lambda k, d, unused: pass_on(k, d).wait_send())
    back(lambda k, d, unused: to_sibling(k, d).wait_send())
    wait_owners(part, p_send)
    if_owner(lambda: wait_all(precv.at[pl.ds(0, count - 1)], o_send))


def body(n, groups, queries, latents, cotangent, comp_weight, sel_idx, sel_count):
    tok = latents.shape[1]
    hop = (WIN + tok - 1) // tok
    assert hop % 2 == 0 and n % 2 == 0
    lead = hop * tok
    cl = tok // CS
    pr = round_up(cl * PIECES, 16)
    nk = round_up(n * SLOT, LANES) + round_up(lead + tok, LANES)
    count = n * groups
    owners = min(CS, count)
    per = CS // owners * SLOT
    dma = pltpu.SemaphoreType.DMA
    reach = hop // 2
    any_spec = pl.BlockSpec(memory_space=pl.ANY)
    vmem_spec = pl.BlockSpec(memory_space=pltpu.VMEM)
    att, qg, lat_grad, weight_grad = pl.pallas_call(
        functools.partial(kernel, n, groups, hop, tok, cl, owners),
        out_shape=(
            jax.ShapeDtypeStruct((tok, H * DL), BF16),
            jax.ShapeDtypeStruct((tok, H * DK), BF16),
            jax.ShapeDtypeStruct((DK, tok), F32),
            jax.ShapeDtypeStruct((CS, DK), F32),
        ),
        in_specs=[
            any_spec,
            any_spec,
            vmem_spec,
            vmem_spec,
            vmem_spec,
            pl.BlockSpec(memory_space=pltpu.SMEM),
        ],
        out_specs=(any_spec, any_spec, vmem_spec, vmem_spec),
        scratch_shapes=[
            pltpu.VMEM((tok, DK), BF16),
            pltpu.VMEM((tok, DK), F32),
            pltpu.VMEM((H * tok, WIDE), BF16),
            pltpu.VMEM((H * tok, DL), BF16),
            pltpu.VMEM((lead, DK), BF16),
            pltpu.VMEM((n, pr, LANES), BF16),
            pltpu.VMEM((pr, LANES), F32),
            pltpu.VMEM((2, nk, WIDE), BF16),
            pltpu.VMEM((nk, WIDE), F32),
            pltpu.VMEM((tok, nk), F32),
            pltpu.VMEM((H * tok, nk), BF16),
            pltpu.VMEM((H * tok, nk), BF16),
            pltpu.VMEM((H * tok, WIDE), F32),
            pltpu.VMEM((tok, H * DL), BF16),
            pltpu.VMEM((tok, H * DK), BF16),
            pltpu.VMEM((n, pr, LANES), F32),
            pltpu.VMEM((n, pr, LANES), BF16),
            pltpu.VMEM((n, pr, LANES), BF16),
            pltpu.VMEM((SLOT, WIDE), F32),
            pltpu.VMEM((CS * SLOT, LANES), F32),
            pltpu.VMEM((count, per, LANES), F32),
            pltpu.VMEM((CS * SLOT, LANES), F32),
            pltpu.VMEM((lead, DK), BF16),
            pltpu.VMEM((reach + 1, tok, DK), BF16),
            pltpu.VMEM((reach, tok, DK), BF16),
            dma((2 * H,)),
            dma((2,)),
            dma,
            dma,
            dma((reach + 1,)),
            dma((reach + 1,)),
            dma((reach + 1,)),
            dma((hop + 1,)),
            dma,
            dma,
            dma((reach + 1,)),
            dma((reach + 1,)),
            dma((reach + 1,)),
            dma((reach + 1,)),
            dma,
            dma,
            dma,
            dma,
        ],
        compiler_params=pltpu.CompilerParams(
            collective_id=0, has_side_effects=True, vmem_limit_bytes=56 * 2**20
        ),
    )(queries[0], cotangent[0], jnp.swapaxes(latents[0], 0, 1), comp_weight, sel_idx[0], sel_count)
    return (att[None], qg[None], jnp.swapaxes(lat_grad, 0, 1)[None], weight_grad)


def solution(mesh):
    in_specs = (
        P("grp", "seq", None),
        P("grp", "seq", None),
        P("grp", "seq", None),
        P(),
        P("grp", "seq", None),
        P("grp", "seq"),
    )
    out_specs = (P("grp", "seq", None), P("grp", "seq", None), P("grp", "seq", None), P())
    return jax.shard_map(
        functools.partial(body, mesh.shape["seq"], mesh.shape["grp"]),
        mesh=mesh,
        in_specs=in_specs,
        out_specs=out_specs,
        check_vma=False,
    )
```

```python
import functools

import jax
import jax.numpy as jnp
from jax import lax
from jax.experimental import pallas as pl
from jax.experimental.pallas import tpu as pltpu
from jax.sharding import PartitionSpec as P

DL = 512
DR = 64
H = 8
QB = 64
CS = 32
WIN = 512
DK = 576
LANES = 128
WIDE = 640
PIECES = WIDE // LANES
SLOT = 8
MASKED = -1e30
UNROLL = 32
INNER = 4

MESH = pl.DeviceIdType.MESH
BF16 = jnp.bfloat16
F32 = jnp.float32
score_scale = 192.0 ** (-0.5)


def round_up(value, step):
    return (value + step - 1) // step * step


def dot_nn(a, b):
    return lax.dot_general(a, b, (((1,), (0,)), ((), ())), preferred_element_type=F32)


def dot_nt(a, b):
    return lax.dot_general(a, b, (((1,), (1,)), ((), ())), preferred_element_type=F32)


def dot_tn(a, b):
    return lax.dot_general(a, b, (((0,), (0,)), ((), ())), preferred_element_type=F32)


def piece_width(j):
    return min(LANES, DK - j * LANES)


def each(size, base, work):
    if size <= UNROLL:
        for k in range(1, size):
            work(lax.rem(base + k, size))
        return

    def one(k, c):
        work(lax.rem(base + k, size))
        return c

    lax.fori_loop(1, size, one, 0)


def kernel(
    n, groups, hop, tok, cl, inner,
    q_ref, cot_ref, lat_t_ref, cw_ref, idx_ref, cnt_ref,
    att_ref, qg_ref, lg_t_ref, wg_ref,
    lat_ref, lg_ref, qq, cc, win, comp, tmp, kk, kf, bias, ds_ref, pp, dq, att_buf, qg_buf,
    pack, cg, crecv_buf, cgrad, part, precv, lines, pout, wing, srecv, wrecv,
    load_sem, save_sem,
    gc_send, gc_recv, gw_send, gw_recv, gs_send, gs_recv,
    rc_send, rc_recv, rs_send, rs_recv, rw_send, rw_recv,
    p_send, p_recv, l_send, l_recv, o_send, o_recv,
):
    seq = lax.axis_index("seq")
    grp = lax.axis_index("grp")
    outer = n // inner
    plane = groups * inner
    depth = seq // inner
    spot = seq % inner
    rank = grp * inner + spot
    parity = seq % 2
    base = seq - parity
    sibling = base + 1 - parity
    own_rows = CS // plane
    nk = bias.shape[1]
    lead = hop * tok
    ext = lead + tok
    cp = nk - round_up(ext, LANES)
    half = (H // 2) * tok
    pair = 2 * DK
    reach = hop // 2

    def in_plane(peer):
        return (lax.div(peer, inner), depth * inner + lax.rem(peer, inner))

    def along(peer):
        return (grp, peer * inner + spot)

    def remote(src, dst, send, recv, device):
        return pltpu.make_async_remote_copy(
            src_ref=src, dst_ref=dst, send_sem=send, recv_sem=recv,
            device_id=device, device_id_type=MESH,
        )

    def wait_all(ref, sem):
        remote(ref, ref, sem, sem, (grp, sibling)).wait_recv()

    def segment(d):
        return pl.ds((hop - d) * tok, tok)

    barrier = pltpu.get_barrier_semaphore()

    def greet(device):
        pl.semaphore_signal(barrier, inc=1, device_id=device, device_id_type=MESH)

    each(n, seq, lambda peer: greet((grp, peer)))
    for g in range(1, groups):
        for i in range(inner):
            greet((lax.rem(grp + g, groups), depth * inner + i))

    loads = []
    for m in range(H // 2):
        for p in range(2):
            rows = pl.ds(p * half + m * tok, tok)
            at = 2 * (2 * m + p)
            loads.append(
                pltpu.make_async_copy(
                    q_ref.at[:, pl.ds(m * pair + p * DL, WIDE)], qq.at[rows], load_sem.at[at]
                )
            )
            loads.append(
                pltpu.make_async_copy(
                    cot_ref.at[:, pl.ds((2 * m + p) * DL, DL)], cc.at[rows], load_sem.at[at + 1]
                )
            )
    for load in loads:
        load.start()

    lat_ref[...] = lat_t_ref[...].astype(F32).T.astype(BF16)
    tmp[...] = jnp.zeros_like(tmp)
    for b in range(cl):
        block = lat_ref[pl.ds(b * CS, CS), :].astype(F32) * cw_ref[...]
        row = jnp.sum(block, axis=0, keepdims=True)
        for j in range(PIECES):
            w = piece_width(j)
            tmp[pl.ds(j * cl + b, 1), pl.ds(0, w)] = row[:, j * LANES : j * LANES + w]
    comp[seq] = tmp[...].astype(BF16)
    pl.semaphore_wait(barrier, n - 1 + (groups - 1) * inner)

    def comp_send(peer):
        return remote(comp.at[seq], comp.at[seq], gc_send, gc_recv, (grp, peer))

    def win_copy(k):
        return remote(
            lat_ref, win.at[segment(2 * k)], gw_send.at[k], gw_recv.at[k],
            (grp, (seq + 2 * k) % n),
        )

    def pass_on(k, d):
        src = lat_ref if k == 0 else win.at[segment(2 * k)]
        return remote(src, win.at[segment(d)], gs_send.at[k], gs_recv.at[d], (grp, sibling))

    def forwarded(work):
        for k in range(reach + 1):
            if k < reach:
                pl.when((parity == 0) & (base >= 2 * k))(lambda k=k: work(k, 2 * k + 1, True))
            if k > 0:
                pl.when((parity == 1) & (base >= 2 * k))(lambda k=k: work(k, 2 * k - 1, False))

    for k in range(reach, 0, -1):
        pl.when(base + 2 * k < n)(lambda k=k: win_copy(k).start())
    pl.when(parity == 0)(lambda: pass_on(0, 1).start())
    each(n, seq, lambda peer: comp_send(peer).start())

    for d in range(1, hop + 1):

        @pl.when(seq < d)
        def _(d=d):
            win[segment(d), :] = jnp.zeros((tok, DK), BF16)

    blocks = tok // QB
    slots = idx_ref.shape[1]
    key_id = lax.broadcasted_iota(jnp.int32, (cp, slots), 0)
    in_slot = key_id % SLOT
    comp_id = jnp.where(in_slot < cl, (key_id // SLOT) * cl + in_slot, -1)
    slot_id = lax.broadcasted_iota(jnp.int32, (cp, slots), 1)
    for r in range(blocks):
        chosen = idx_ref[pl.ds(r, 1), :]
        hit = (comp_id == chosen) & (slot_id < cnt_ref[0, r])
        hit = jnp.where(hit, 1.0, 0.0).astype(BF16)
        live = dot_nt(jnp.ones((QB, slots), BF16), hit)
        bias[pl.ds(r * QB, QB), pl.ds(0, cp)] = jnp.where(live > 0.5, 0.0, MASKED)
    wide = nk - cp
    row = lax.broadcasted_iota(jnp.int32, (tok, wide), 0)
    col = lax.broadcasted_iota(jnp.int32, (tok, wide), 1)
    shift = lead - WIN
    ok = (col > row + shift) & (col <= row + lead) & (col - lead + seq * tok >= 0)
    bias[:, pl.ds(cp, wide)] = jnp.where(ok, 0.0, MASKED)
    kf[pl.ds(0, cp), :] = jnp.zeros((cp, WIDE), F32)
    if nk > cp + ext:
        kk[:, pl.ds(cp + ext, nk - cp - ext), :] = jnp.zeros((2, nk - cp - ext, WIDE), BF16)

    def lay_out(d, value):
        rows = pl.ds(cp + (hop - d) * tok, tok)
        padded = jnp.concatenate(
            [value.astype(F32), jnp.zeros((tok, WIDE - DK), F32)], axis=1
        )
        kk[0, rows, :] = padded.astype(BF16)
        kk[1, rows, :] = pltpu.roll(padded, DR, 1).astype(BF16)

    lay_out(0, lat_ref[...])
    pack[...] = jnp.zeros_like(pack)
    part[...] = jnp.zeros_like(part)

    for k in range(1, reach + 1):

        @pl.when(base >= 2 * k)
        def _(k=k):
            win_copy(k).wait_recv()
            if k < reach:
                pl.when(parity == 0)(lambda: pass_on(k, 2 * k + 1).start())
            pl.when(parity == 1)(lambda: pass_on(k, 2 * k - 1).start())

    for k in range(1, reach + 1):
        lay_out(2 * k, win[segment(2 * k), :])
    wait_all(comp.at[pl.ds(0, n - 1)], gc_recv)

    def unpack(o, c):
        packed = comp[o].astype(F32)
        for j in range(PIECES):
            kf[pl.ds(pl.multiple_of(o * SLOT, SLOT), cl), pl.ds(j * LANES, LANES)] = packed[
                j * cl : (j + 1) * cl, :
            ]
        return c

    lax.fori_loop(0, n, unpack, 0)
    kk[0, pl.ds(0, cp), :] = kf[pl.ds(0, cp), :].astype(BF16)
    kk[1, pl.ds(0, cp), :] = pltpu.roll(kf[pl.ds(0, cp), :], DR, 1).astype(BF16)

    def sibling_arrival(k, d):
        pass_on(k, d).wait_recv()

    for k in range(reach + 1):
        if k < reach:
            pl.when((parity == 1) & (base >= 2 * k))(lambda k=k: sibling_arrival(k, 2 * k + 1))
        if k > 0:
            pl.when((parity == 0) & (base >= 2 * k))(lambda k=k: sibling_arrival(k, 2 * k - 1))
    for d in range(1, hop + 1, 2):
        lay_out(d, win[segment(d), :])
    for load in loads:
        load.wait()

    step = min(256, half)
    heads = step // tok
    for c in range(2 * half // step):
        p = c * step // half
        rows = pl.ds(c * step, step)
        keys = kk[p]
        values = kk[0, :, pl.ds(0, DL)]
        s = dot_nt(qq[rows, :], keys) * score_scale
        s = (s.reshape(heads, tok, nk) + bias[...][None]).reshape(step, nk)
        e = jnp.exp(s - jnp.max(s, axis=1, keepdims=True))
        w = e * (1.0 / jnp.sum(e, axis=1, keepdims=True))
        rounded = w.astype(BF16)
        pp[rows, :] = rounded
        context = dot_nn(rounded, values)
        grads = cc[rows, :]
        row_dot = jnp.sum(grads.astype(F32) * context, axis=1, keepdims=True)
        dscore = (w * (dot_nt(grads, values) - row_dot)).astype(BF16)
        ds_ref[rows, :] = dscore
        dq[rows, :] = dot_nn(dscore, keys) * score_scale
        for i in range(heads):
            m = (c * step - p * half) // tok + i
            att_buf[:, pl.ds((2 * m + p) * DL, DL)] = context[i * tok : (i + 1) * tok].astype(BF16)

    save_att = pltpu.make_async_copy(att_buf, att_ref, save_sem.at[0])
    save_att.start()

    def key_pass(start):
        size = min(256, nk - start)
        cols = pl.ds(start, size)
        even = dot_tn(ds_ref[pl.ds(0, half), cols], qq[pl.ds(0, half), :])
        odd = dot_tn(ds_ref[pl.ds(half, half), cols], qq[pl.ds(half, half), :])
        value = dot_tn(pp[:, cols], cc[...])
        total = (even + pltpu.roll(odd, WIDE - DR, 1)) * score_scale
        kf[cols, pl.ds(0, DL)] = total[:, :DL] + value
        kf[cols, pl.ds(DL, LANES)] = total[:, DL:]

    def seg_grad(d):
        return kf[pl.ds(cp + (hop - d) * tok, tok), pl.ds(0, DK)]

    def sum_send(peer):
        return remote(cg.at[peer], crecv_buf.at[seq], rc_send, rc_recv, (grp, peer))

    def to_sibling(k, d):
        return remote(
            wing.at[segment(d)], srecv.at[k], rs_send.at[k], rs_recv.at[k], (grp, sibling)
        )

    def to_source(k):
        return remote(
            wing.at[segment(2 * k)], wrecv.at[k - 1], rw_send.at[k], rw_recv.at[k],
            (grp, (seq + n - 2 * k) % n),
        )

    def part_copy(peer):
        return remote(part.at[peer], precv.at[rank], p_send, p_recv, in_plane(peer))

    def line_copy(peer):
        return remote(lines.at[depth], lines.at[depth], l_send, l_recv, along(peer))

    def out_copy(peer):
        return remote(pout.at[rank], pout.at[rank], o_send, o_recv, in_plane(peer))

    done = 0
    while done < cp:
        key_pass(done)
        done += 256

    def pack_one(o, c):
        for j in range(PIECES):
            pack[o, pl.ds(j * cl, cl), :] = kf[
                pl.ds(pl.multiple_of(o * SLOT, SLOT), cl), pl.ds(j * LANES, LANES)
            ]
        return c

    lax.fori_loop(0, n, pack_one, 0)
    cg[...] = pack[...].astype(BF16)
    crecv_buf[seq] = cg[seq]
    each(n, seq, lambda peer: sum_send(peer).start())

    def send_sibling(k, d):
        wing[segment(d), :] = seg_grad(d).astype(BF16)
        to_sibling(k, d).start()

    def back(work):
        for k in range(reach, -1, -1):
            if k > 0:
                pl.when((parity == 0) & (base >= 2 * k))(lambda k=k: work(k, 2 * k - 1, True))
            if k < reach:
                pl.when((parity == 1) & (base >= 2 * k))(lambda k=k: work(k, 2 * k + 1, False))

    def ship(d):
        if d == hop:

            @pl.when((parity == 0) & (base >= hop))
            def _():
                wing[segment(hop), :] = seg_grad(hop).astype(BF16)
                to_source(reach).start()

        elif d % 2 == 1:
            k = (d + 1) // 2
            pl.when((parity == 0) & (base >= 2 * k))(lambda: send_sibling(k, d))
            pl.when((parity == 1) & (base >= 2 * k - 2))(lambda: send_sibling(k - 1, d))

    ready = hop
    while True:
        while ready > 0 and cp + (hop - ready + 1) * tok <= done:
            ship(ready)
            ready -= 1
        if done >= nk:
            break
        key_pass(done)
        done += 256

    wait_all(crecv_buf.at[pl.ds(0, n - 1)], rc_recv)
    total = jnp.sum(crecv_buf[...].astype(F32), axis=0)
    for j in range(PIECES):
        cgrad[pl.ds(0, cl), pl.ds(j * LANES, LANES)] = total[j * cl : (j + 1) * cl, :]
    weight = jnp.zeros((CS, DK), F32)
    for b in range(cl):
        weight = weight + cgrad[pl.ds(b, 1), pl.ds(0, DK)] * lat_ref[pl.ds(b * CS, CS), :].astype(F32)
    for o in range(plane):
        for j in range(PIECES):
            w = piece_width(j)
            part[o, pl.ds(j * own_rows, own_rows), pl.ds(0, w)] = weight[
                o * own_rows : (o + 1) * own_rows, j * LANES : j * LANES + w
            ]
    each(plane, rank, lambda peer: part_copy(peer).start())
    precv[rank] = part[rank]

    wait_all(precv.at[pl.ds(0, plane - 1)], p_recv)
    lines[depth] = jnp.sum(precv[...], axis=0)
    each(outer, depth, lambda peer: line_copy(peer).start())

    def merge(k):
        to_sibling(k, 1).wait_recv()
        wing[segment(2 * k), :] = (seg_grad(2 * k) + srecv[k].astype(F32)).astype(BF16)
        to_source(k).start()

    for k in range(reach, 0, -1):
        if k < reach:
            pl.when(base >= 2 * k)(lambda k=k: merge(k))
        else:
            pl.when((parity == 1) & (base >= 2 * k))(lambda k=k: merge(k))

    wait_all(lines.at[pl.ds(0, outer - 1)], l_recv)
    pout[rank] = jnp.sum(lines[...], axis=0)
    each(plane, rank, lambda peer: out_copy(peer).start())

    for m in range(H // 2):
        even = pl.ds(m * tok, tok)
        odd = pl.ds(half + m * tok, tok)
        qg_buf[:, pl.ds(m * pair, DL)] = dq[even, pl.ds(0, DL)].astype(BF16)
        qg_buf[:, pl.ds(m * pair + DL, LANES)] = (
            dq[even, pl.ds(DL, LANES)] + dq[odd, pl.ds(0, LANES)]
        ).astype(BF16)
        qg_buf[:, pl.ds(m * pair + WIDE, DL)] = dq[odd, pl.ds(LANES, DL)].astype(BF16)
    save_qg = pltpu.make_async_copy(qg_buf, qg_ref, save_sem.at[1])
    save_qg.start()

    own = seg_grad(0)
    for b in range(cl):
        rows = pl.ds(b * CS, CS)
        lg_ref[rows, :] = own[b * CS : (b + 1) * CS] + cw_ref[...] * cgrad[pl.ds(b, 1), pl.ds(0, DK)]

    @pl.when(parity == 0)
    def _():
        to_sibling(0, 1).wait_recv()
        lg_ref[...] += srecv[0].astype(F32)

    for k in range(1, reach + 1):

        @pl.when(base + 2 * k < n)
        def _(k=k):
            to_source(k).wait_recv()
            lg_ref[...] += wrecv[k - 1].astype(F32)

    lg_t_ref[...] = lg_ref[...].T
    wait_all(pout.at[pl.ds(0, plane - 1)], o_recv)
    for o in range(plane):
        for j in range(PIECES):
            w = piece_width(j)
            wg_ref[pl.ds(o * own_rows, own_rows), pl.ds(j * LANES, w)] = pout[
                o, pl.ds(j * own_rows, own_rows), pl.ds(0, w)
            ]

    save_att.wait()
    save_qg.wait()
    wait_all(comp.at[pl.ds(0, n - 1)], gc_send)
    wait_all(cg.at[pl.ds(0, n - 1)], rc_send)
    for k in range(1, reach + 1):
        pl.when(base + 2 * k < n)(lambda k=k: win_copy(k).wait_send())
        pl.when(base >= 2 * k)(lambda k=k: to_source(k).wait_send())
    forwarded(lambda k, d, unused: pass_on(k, d).wait_send())
    back(lambda k, d, unused: to_sibling(k, d).wait_send())
    wait_all(part.at[pl.ds(0, plane - 1)], p_send)
    wait_all(lines.at[pl.ds(0, outer - 1)], l_send)
    wait_all(pout.at[pl.ds(0, plane - 1)], o_send)


def body(n, groups, queries, latents, cotangent, comp_weight, sel_idx, sel_count):
    tok = latents.shape[1]
    hop = (WIN + tok - 1) // tok
    assert hop % 2 == 0 and n % 2 == 0
    lead = hop * tok
    cl = tok // CS
    pr = round_up(cl * PIECES, 16)
    nk = round_up(n * SLOT, LANES) + round_up(lead + tok, LANES)
    inner = INNER
    plane = groups * inner
    assert n % inner == 0 and CS % plane == 0
    own_pack = round_up(CS // plane * PIECES, SLOT)
    dma = pltpu.SemaphoreType.DMA
    reach = hop // 2
    any_spec = pl.BlockSpec(memory_space=pl.ANY)
    hbm_spec = pl.BlockSpec(memory_space=pltpu.HBM)
    vmem_spec = pl.BlockSpec(memory_space=pltpu.VMEM)
    att, qg, lat_grad, weight_grad = pl.pallas_call(
        functools.partial(kernel, n, groups, hop, tok, cl, inner),
        out_shape=(
            jax.ShapeDtypeStruct((tok, H * DL), BF16),
            jax.ShapeDtypeStruct((tok, H * DK), BF16),
            jax.ShapeDtypeStruct((DK, tok), F32),
            jax.ShapeDtypeStruct((CS, DK), F32),
        ),
        in_specs=[
            hbm_spec,
            hbm_spec,
            vmem_spec,
            vmem_spec,
            vmem_spec,
            pl.BlockSpec(memory_space=pltpu.SMEM),
        ],
        out_specs=(any_spec, any_spec, vmem_spec, vmem_spec),
        scratch_shapes=[
            pltpu.VMEM((tok, DK), BF16),
            pltpu.VMEM((tok, DK), F32),
            pltpu.VMEM((H * tok, WIDE), BF16),
            pltpu.VMEM((H * tok, DL), BF16),
            pltpu.VMEM((lead, DK), BF16),
            pltpu.VMEM((n, pr, LANES), BF16),
            pltpu.VMEM((pr, LANES), F32),
            pltpu.VMEM((2, nk, WIDE), BF16),
            pltpu.VMEM((nk, WIDE), F32),
            pltpu.VMEM((tok, nk), F32),
            pltpu.VMEM((H * tok, nk), BF16),
            pltpu.VMEM((H * tok, nk), BF16),
            pltpu.VMEM((H * tok, WIDE), F32),
            pltpu.VMEM((tok, H * DL), BF16),
            pltpu.VMEM((tok, H * DK), BF16),
            pltpu.VMEM((n, pr, LANES), F32),
            pltpu.VMEM((n, pr, LANES), BF16),
            pltpu.VMEM((n, pr, LANES), BF16),
            pltpu.VMEM((SLOT, WIDE), F32),
            pltpu.VMEM((plane, own_pack, LANES), F32),
            pltpu.VMEM((plane, own_pack, LANES), F32),
            pltpu.VMEM((n // inner, own_pack, LANES), F32),
            pltpu.VMEM((plane, own_pack, LANES), F32),
            pltpu.VMEM((lead, DK), BF16),
            pltpu.VMEM((reach + 1, tok, DK), BF16),
            pltpu.VMEM((reach, tok, DK), BF16),
            dma((2 * H,)),
            dma((2,)),
            dma,
            dma,
            dma((reach + 1,)),
            dma((reach + 1,)),
            dma((reach + 1,)),
            dma((hop + 1,)),
            dma,
            dma,
            dma((reach + 1,)),
            dma((reach + 1,)),
            dma((reach + 1,)),
            dma((reach + 1,)),
            dma,
            dma,
            dma,
            dma,
            dma,
            dma,
        ],
        compiler_params=pltpu.CompilerParams(
            collective_id=0, has_side_effects=True, vmem_limit_bytes=32 * 2**20
        ),
    )(queries[0], cotangent[0], jnp.swapaxes(latents[0], 0, 1), comp_weight, sel_idx[0], sel_count)
    return (att[None], qg[None], jnp.swapaxes(lat_grad, 0, 1)[None], weight_grad)


def solution(mesh):
    in_specs = (
        P("grp", "seq", None),
        P("grp", "seq", None),
        P("grp", "seq", None),
        P(),
        P("grp", "seq", None),
        P("grp", "seq"),
    )
    out_specs = (P("grp", "seq", None), P("grp", "seq", None), P("grp", "seq", None), P())
    return jax.shard_map(
        functools.partial(body, mesh.shape["seq"], mesh.shape["grp"]),
        mesh=mesh,
        in_specs=in_specs,
        out_specs=out_specs,
        check_vma=False,
    )
```

```python
import functools

import jax
import jax.numpy as jnp
from jax import lax
from jax.experimental import pallas as pl
from jax.experimental.pallas import tpu as pltpu
from jax.sharding import PartitionSpec as P

DL = 512
DR = 64
H = 8
QB = 64
CS = 32
WIN = 512
DK = 576
LANES = 128
WIDE = 640
PIECES = WIDE // LANES
SLOT = 8
MASKED = -1e30
UNROLL = 32
INNER = 4

MESH = pl.DeviceIdType.MESH
BF16 = jnp.bfloat16
F32 = jnp.float32
score_scale = 192.0 ** (-0.5)


def round_up(value, step):
    return (value + step - 1) // step * step


def dot_nn(a, b):
    return lax.dot_general(a, b, (((1,), (0,)), ((), ())), preferred_element_type=F32)


def dot_nt(a, b):
    return lax.dot_general(a, b, (((1,), (1,)), ((), ())), preferred_element_type=F32)


def dot_tn(a, b):
    return lax.dot_general(a, b, (((0,), (0,)), ((), ())), preferred_element_type=F32)


def piece_width(j):
    return min(LANES, DK - j * LANES)


def each(size, base, work):
    if size <= UNROLL:
        for k in range(1, size):
            work(lax.rem(base + k, size))
        return

    def one(k, c):
        work(lax.rem(base + k, size))
        return c

    lax.fori_loop(1, size, one, 0)


def kernel(
    n, groups, hop, tok, cl, inner,
    q_ref, cot_ref, lat_t_ref, cw_ref, idx_ref, cnt_ref,
    att_ref, qg_ref, lg_t_ref, wg_ref,
    lat_ref, lg_ref, qq, cc, win, comp, tmp, kk, kf, bias, ds_ref, pp, dq, att_buf, qg_buf,
    pack, cg, crecv_buf, cgrad, part, precv, lines, pout, wing, srecv, wrecv,
    load_sem, save_sem,
    gc_send, gc_recv, gw_send, gw_recv, gs_send, gs_recv,
    rc_send, rc_recv, rs_send, rs_recv, rw_send, rw_recv,
    p_send, p_recv, l_send, l_recv, o_send, o_recv,
):
    seq = lax.axis_index("seq")
    grp = lax.axis_index("grp")
    outer = n // inner
    plane = groups * inner
    depth = seq // inner
    spot = seq % inner
    rank = grp * inner + spot
    parity = seq % 2
    base = seq - parity
    sibling = base + 1 - parity
    own_rows = CS // plane
    nk = bias.shape[1]
    lead = hop * tok
    ext = lead + tok
    cp = nk - round_up(ext, LANES)
    half = (H // 2) * tok
    pair = 2 * DK
    reach = hop // 2

    def in_plane(peer):
        return (lax.div(peer, inner), depth * inner + lax.rem(peer, inner))

    def along(peer):
        return (grp, peer * inner + spot)

    def remote(src, dst, send, recv, device):
        return pltpu.make_async_remote_copy(
            src_ref=src, dst_ref=dst, send_sem=send, recv_sem=recv,
            device_id=device, device_id_type=MESH,
        )

    def wait_all(ref, sem):
        remote(ref, ref, sem, sem, (grp, sibling)).wait_recv()

    def segment(d):
        return pl.ds((hop - d) * tok, tok)

    barrier = pltpu.get_barrier_semaphore()

    def greet(device):
        pl.semaphore_signal(barrier, inc=1, device_id=device, device_id_type=MESH)

    each(n, seq, lambda peer: greet((grp, peer)))
    for g in range(1, groups):
        for i in range(inner):
            greet((lax.rem(grp + g, groups), depth * inner + i))

    loads = []
    for m in range(H // 2):
        for p in range(2):
            rows = pl.ds(p * half + m * tok, tok)
            at = 2 * (2 * m + p)
            loads.append(
                pltpu.make_async_copy(
                    q_ref.at[:, pl.ds(m * pair + p * DL, WIDE)], qq.at[rows], load_sem.at[at]
                )
            )
            loads.append(
                pltpu.make_async_copy(
                    cot_ref.at[:, pl.ds((2 * m + p) * DL, DL)], cc.at[rows], load_sem.at[at + 1]
                )
            )
    for load in loads:
        load.start()

    lat_ref[...] = lat_t_ref[...].astype(F32).T.astype(BF16)
    tmp[...] = jnp.zeros_like(tmp)
    for b in range(cl):
        block = lat_ref[pl.ds(b * CS, CS), :].astype(F32) * cw_ref[...]
        row = jnp.sum(block, axis=0, keepdims=True)
        for j in range(PIECES):
            w = piece_width(j)
            tmp[pl.ds(j * cl + b, 1), pl.ds(0, w)] = row[:, j * LANES : j * LANES + w]
    comp[seq] = tmp[...].astype(BF16)
    pl.semaphore_wait(barrier, n - 1 + (groups - 1) * inner)

    def comp_send(peer):
        return remote(comp.at[seq], comp.at[seq], gc_send, gc_recv, (grp, peer))

    def win_copy(k):
        return remote(
            lat_ref, win.at[segment(2 * k)], gw_send.at[k], gw_recv.at[k],
            (grp, (seq + 2 * k) % n),
        )

    def pass_on(k, d):
        src = lat_ref if k == 0 else win.at[segment(2 * k)]
        return remote(src, win.at[segment(d)], gs_send.at[k], gs_recv.at[d], (grp, sibling))

    def forwarded(work):
        for k in range(reach + 1):
            if k < reach:
                pl.when((parity == 0) & (base >= 2 * k))(lambda k=k: work(k, 2 * k + 1, True))
            if k > 0:
                pl.when((parity == 1) & (base >= 2 * k))(lambda k=k: work(k, 2 * k - 1, False))

    for k in range(reach, 0, -1):
        pl.when(base + 2 * k < n)(lambda k=k: win_copy(k).start())
    pl.when(parity == 0)(lambda: pass_on(0, 1).start())
    each(n, seq, lambda peer: comp_send(peer).start())

    for d in range(1, hop + 1):

        @pl.when(seq < d)
        def _(d=d):
            win[segment(d), :] = jnp.zeros((tok, DK), BF16)

    blocks = tok // QB
    slots = idx_ref.shape[1]
    key_id = lax.broadcasted_iota(jnp.int32, (cp, slots), 0)
    in_slot = key_id % SLOT
    comp_id = jnp.where(in_slot < cl, (key_id // SLOT) * cl + in_slot, -1)
    slot_id = lax.broadcasted_iota(jnp.int32, (cp, slots), 1)
    for r in range(blocks):
        chosen = idx_ref[pl.ds(r, 1), :]
        hit = (comp_id == chosen) & (slot_id < cnt_ref[0, r])
        hit = jnp.where(hit, 1.0, 0.0).astype(BF16)
        live = dot_nt(jnp.ones((QB, slots), BF16), hit)
        bias[pl.ds(r * QB, QB), pl.ds(0, cp)] = jnp.where(live > 0.5, 0.0, MASKED)
    wide = nk - cp
    row = lax.broadcasted_iota(jnp.int32, (tok, wide), 0)
    col = lax.broadcasted_iota(jnp.int32, (tok, wide), 1)
    shift = lead - WIN
    ok = (col > row + shift) & (col <= row + lead) & (col - lead + seq * tok >= 0)
    bias[:, pl.ds(cp, wide)] = jnp.where(ok, 0.0, MASKED)
    kf[pl.ds(0, cp), :] = jnp.zeros((cp, WIDE), F32)
    if nk > cp + ext:
        kk[:, pl.ds(cp + ext, nk - cp - ext), :] = jnp.zeros((2, nk - cp - ext, WIDE), BF16)

    def lay_out(d, value):
        rows = pl.ds(cp + (hop - d) * tok, tok)
        padded = jnp.concatenate(
            [value.astype(F32), jnp.zeros((tok, WIDE - DK), F32)], axis=1
        )
        kk[0, rows, :] = padded.astype(BF16)
        kk[1, rows, :] = pltpu.roll(padded, DR, 1).astype(BF16)

    lay_out(0, lat_ref[...])
    pack[...] = jnp.zeros_like(pack)
    part[...] = jnp.zeros_like(part)

    for k in range(1, reach + 1):

        @pl.when(base >= 2 * k)
        def _(k=k):
            win_copy(k).wait_recv()
            if k < reach:
                pl.when(parity == 0)(lambda: pass_on(k, 2 * k + 1).start())
            pl.when(parity == 1)(lambda: pass_on(k, 2 * k - 1).start())

    for k in range(1, reach + 1):
        lay_out(2 * k, win[segment(2 * k), :])
    wait_all(comp.at[pl.ds(0, n - 1)], gc_recv)

    def unpack(o, c):
        packed = comp[o].astype(F32)
        for j in range(PIECES):
            kf[pl.ds(pl.multiple_of(o * SLOT, SLOT), cl), pl.ds(j * LANES, LANES)] = packed[
                j * cl : (j + 1) * cl, :
            ]
        return c

    lax.fori_loop(0, n, unpack, 0)
    kk[0, pl.ds(0, cp), :] = kf[pl.ds(0, cp), :].astype(BF16)
    kk[1, pl.ds(0, cp), :] = pltpu.roll(kf[pl.ds(0, cp), :], DR, 1).astype(BF16)

    def sibling_arrival(k, d):
        pass_on(k, d).wait_recv()

    for k in range(reach + 1):
        if k < reach:
            pl.when((parity == 1) & (base >= 2 * k))(lambda k=k: sibling_arrival(k, 2 * k + 1))
        if k > 0:
            pl.when((parity == 0) & (base >= 2 * k))(lambda k=k: sibling_arrival(k, 2 * k - 1))
    for d in range(1, hop + 1, 2):
        lay_out(d, win[segment(d), :])
    for load in loads:
        load.wait()

    step = min(256, half)
    heads = step // tok
    for c in range(2 * half // step):
        p = c * step // half
        rows = pl.ds(c * step, step)
        keys = kk[p]
        values = kk[0, :, pl.ds(0, DL)]
        s = dot_nt(qq[rows, :], keys) * score_scale
        s = (s.reshape(heads, tok, nk) + bias[...][None]).reshape(step, nk)
        e = jnp.exp(s - jnp.max(s, axis=1, keepdims=True))
        w = e * (1.0 / jnp.sum(e, axis=1, keepdims=True))
        rounded = w.astype(BF16)
        pp[rows, :] = rounded
        context = dot_nn(rounded, values)
        grads = cc[rows, :]
        row_dot = jnp.sum(grads.astype(F32) * context, axis=1, keepdims=True)
        dscore = (w * (dot_nt(grads, values) - row_dot)).astype(BF16)
        ds_ref[rows, :] = dscore
        dq[rows, :] = dot_nn(dscore, keys) * score_scale
        for i in range(heads):
            m = (c * step - p * half) // tok + i
            att_buf[:, pl.ds((2 * m + p) * DL, DL)] = context[i * tok : (i + 1) * tok].astype(BF16)

    save_att = pltpu.make_async_copy(att_buf, att_ref, save_sem.at[0])
    save_att.start()

    def key_pass(start):
        size = min(256, nk - start)
        cols = pl.ds(start, size)
        even = dot_tn(ds_ref[pl.ds(0, half), cols], qq[pl.ds(0, half), :])
        odd = dot_tn(ds_ref[pl.ds(half, half), cols], qq[pl.ds(half, half), :])
        value = dot_tn(pp[:, cols], cc[...])
        total = (even + pltpu.roll(odd, WIDE - DR, 1)) * score_scale
        kf[cols, pl.ds(0, DL)] = total[:, :DL] + value
        kf[cols, pl.ds(DL, LANES)] = total[:, DL:]

    def seg_grad(d):
        return kf[pl.ds(cp + (hop - d) * tok, tok), pl.ds(0, DK)]

    def sum_send(peer):
        return remote(cg.at[peer], crecv_buf.at[seq], rc_send, rc_recv, (grp, peer))

    def to_sibling(k, d):
        return remote(
            wing.at[segment(d)], srecv.at[k], rs_send.at[k], rs_recv.at[k], (grp, sibling)
        )

    def to_source(k):
        return remote(
            wing.at[segment(2 * k)], wrecv.at[k - 1], rw_send.at[k], rw_recv.at[k],
            (grp, (seq + n - 2 * k) % n),
        )

    def part_copy(peer):
        return remote(part.at[peer], precv.at[rank], p_send, p_recv, in_plane(peer))

    def line_copy(peer):
        return remote(lines.at[depth], lines.at[depth], l_send, l_recv, along(peer))

    def out_copy(peer):
        return remote(pout.at[rank], pout.at[rank], o_send, o_recv, in_plane(peer))

    done = 0
    while done < cp:
        key_pass(done)
        done += 256

    def pack_one(o, c):
        for j in range(PIECES):
            pack[o, pl.ds(j * cl, cl), :] = kf[
                pl.ds(pl.multiple_of(o * SLOT, SLOT), cl), pl.ds(j * LANES, LANES)
            ]
        return c

    lax.fori_loop(0, n, pack_one, 0)
    cg[...] = pack[...].astype(BF16)
    crecv_buf[seq] = cg[seq]
    each(n, seq, lambda peer: sum_send(peer).start())

    def send_sibling(k, d):
        wing[segment(d), :] = seg_grad(d).astype(BF16)
        to_sibling(k, d).start()

    def back(work):
        for k in range(reach, -1, -1):
            if k > 0:
                pl.when((parity == 0) & (base >= 2 * k))(lambda k=k: work(k, 2 * k - 1, True))
            if k < reach:
                pl.when((parity == 1) & (base >= 2 * k))(lambda k=k: work(k, 2 * k + 1, False))

    def ship(d):
        if d == hop:

            @pl.when((parity == 0) & (base >= hop))
            def _():
                wing[segment(hop), :] = seg_grad(hop).astype(BF16)
                to_source(reach).start()

        elif d % 2 == 1:
            k = (d + 1) // 2
            pl.when((parity == 0) & (base >= 2 * k))(lambda: send_sibling(k, d))
            pl.when((parity == 1) & (base >= 2 * k - 2))(lambda: send_sibling(k - 1, d))

    ready = hop
    while True:
        while ready > 0 and cp + (hop - ready + 1) * tok <= done:
            ship(ready)
            ready -= 1
        if done >= nk:
            break
        key_pass(done)
        done += 256

    wait_all(crecv_buf.at[pl.ds(0, n - 1)], rc_recv)
    total = jnp.sum(crecv_buf[...].astype(F32), axis=0)
    for j in range(PIECES):
        cgrad[pl.ds(0, cl), pl.ds(j * LANES, LANES)] = total[j * cl : (j + 1) * cl, :]
    weight = jnp.zeros((CS, DK), F32)
    for b in range(cl):
        weight = weight + cgrad[pl.ds(b, 1), pl.ds(0, DK)] * lat_ref[pl.ds(b * CS, CS), :].astype(F32)
    for o in range(plane):
        for j in range(PIECES):
            w = piece_width(j)
            part[o, pl.ds(j * own_rows, own_rows), pl.ds(0, w)] = weight[
                o * own_rows : (o + 1) * own_rows, j * LANES : j * LANES + w
            ]
    each(plane, rank, lambda peer: part_copy(peer).start())
    precv[rank] = part[rank]

    wait_all(precv.at[pl.ds(0, plane - 1)], p_recv)
    lines[depth] = jnp.sum(precv[...], axis=0)
    each(outer, depth, lambda peer: line_copy(peer).start())

    def merge(k):
        to_sibling(k, 1).wait_recv()
        wing[segment(2 * k), :] = (seg_grad(2 * k) + srecv[k].astype(F32)).astype(BF16)
        to_source(k).start()

    for k in range(reach, 0, -1):
        if k < reach:
            pl.when(base >= 2 * k)(lambda k=k: merge(k))
        else:
            pl.when((parity == 1) & (base >= 2 * k))(lambda k=k: merge(k))

    wait_all(lines.at[pl.ds(0, outer - 1)], l_recv)
    pout[rank] = jnp.sum(lines[...], axis=0)
    each(plane, rank, lambda peer: out_copy(peer).start())

    for m in range(H // 2):
        even = pl.ds(m * tok, tok)
        odd = pl.ds(half + m * tok, tok)
        qg_buf[:, pl.ds(m * pair, DL)] = dq[even, pl.ds(0, DL)].astype(BF16)
        qg_buf[:, pl.ds(m * pair + DL, LANES)] = (
            dq[even, pl.ds(DL, LANES)] + dq[odd, pl.ds(0, LANES)]
        ).astype(BF16)
        qg_buf[:, pl.ds(m * pair + WIDE, DL)] = dq[odd, pl.ds(LANES, DL)].astype(BF16)
    save_qg = pltpu.make_async_copy(qg_buf, qg_ref, save_sem.at[1])
    save_qg.start()

    own = seg_grad(0)
    for b in range(cl):
        rows = pl.ds(b * CS, CS)
        lg_ref[rows, :] = own[b * CS : (b + 1) * CS] + cw_ref[...] * cgrad[pl.ds(b, 1), pl.ds(0, DK)]

    @pl.when(parity == 0)
    def _():
        to_sibling(0, 1).wait_recv()
        lg_ref[...] += srecv[0].astype(F32)

    for k in range(1, reach + 1):

        @pl.when(base + 2 * k < n)
        def _(k=k):
            to_source(k).wait_recv()
            lg_ref[...] += wrecv[k - 1].astype(F32)

    lg_t_ref[...] = lg_ref[...].T
    wait_all(pout.at[pl.ds(0, plane - 1)], o_recv)
    for o in range(plane):
        for j in range(PIECES):
            w = piece_width(j)
            wg_ref[pl.ds(o * own_rows, own_rows), pl.ds(j * LANES, w)] = pout[
                o, pl.ds(j * own_rows, own_rows), pl.ds(0, w)
            ]

    save_att.wait()
    save_qg.wait()
    wait_all(comp.at[pl.ds(0, n - 1)], gc_send)
    wait_all(cg.at[pl.ds(0, n - 1)], rc_send)
    for k in range(1, reach + 1):
        pl.when(base + 2 * k < n)(lambda k=k: win_copy(k).wait_send())
        pl.when(base >= 2 * k)(lambda k=k: to_source(k).wait_send())
    forwarded(lambda k, d, unused: pass_on(k, d).wait_send())
    back(lambda k, d, unused: to_sibling(k, d).wait_send())
    wait_all(part.at[pl.ds(0, plane - 1)], p_send)
    wait_all(lines.at[pl.ds(0, outer - 1)], l_send)
    wait_all(pout.at[pl.ds(0, plane - 1)], o_send)


def body(n, groups, queries, latents, cotangent, comp_weight, sel_idx, sel_count):
    tok = latents.shape[1]
    hop = (WIN + tok - 1) // tok
    assert hop % 2 == 0 and n % 2 == 0
    lead = hop * tok
    cl = tok // CS
    pr = round_up(cl * PIECES, 16)
    nk = round_up(n * SLOT, LANES) + round_up(lead + tok, LANES)
    inner = INNER
    plane = groups * inner
    assert n % inner == 0 and CS % plane == 0
    own_pack = round_up(CS // plane * PIECES, SLOT)
    dma = pltpu.SemaphoreType.DMA
    reach = hop // 2
    any_spec = pl.BlockSpec(memory_space=pl.ANY)
    hbm_spec = pl.BlockSpec(memory_space=pltpu.HBM)
    vmem_spec = pl.BlockSpec(memory_space=pltpu.VMEM)
    att, qg, lat_grad, weight_grad = pl.pallas_call(
        functools.partial(kernel, n, groups, hop, tok, cl, inner),
        out_shape=(
            jax.ShapeDtypeStruct((tok, H * DL), BF16),
            jax.ShapeDtypeStruct((tok, H * DK), BF16),
            jax.ShapeDtypeStruct((DK, tok), F32),
            jax.ShapeDtypeStruct((CS, DK), F32),
        ),
        in_specs=[
            hbm_spec,
            hbm_spec,
            vmem_spec,
            vmem_spec,
            vmem_spec,
            pl.BlockSpec(memory_space=pltpu.SMEM),
        ],
        out_specs=(any_spec, any_spec, vmem_spec, vmem_spec),
        scratch_shapes=[
            pltpu.VMEM((tok, DK), BF16),
            pltpu.VMEM((tok, DK), F32),
            pltpu.VMEM((H * tok, WIDE), BF16),
            pltpu.VMEM((H * tok, DL), BF16),
            pltpu.VMEM((lead, DK), BF16),
            pltpu.VMEM((n, pr, LANES), BF16),
            pltpu.VMEM((pr, LANES), F32),
            pltpu.VMEM((2, nk, WIDE), BF16),
            pltpu.VMEM((nk, WIDE), F32),
            pltpu.VMEM((tok, nk), F32),
            pltpu.VMEM((H * tok, nk), BF16),
            pltpu.VMEM((H * tok, nk), BF16),
            pltpu.VMEM((H * tok, WIDE), F32),
            pltpu.VMEM((tok, H * DL), BF16),
            pltpu.VMEM((tok, H * DK), BF16),
            pltpu.VMEM((n, pr, LANES), F32),
            pltpu.VMEM((n, pr, LANES), BF16),
            pltpu.VMEM((n, pr, LANES), BF16),
            pltpu.VMEM((SLOT, WIDE), F32),
            pltpu.VMEM((plane, own_pack, LANES), F32),
            pltpu.VMEM((plane, own_pack, LANES), F32),
            pltpu.VMEM((n // inner, own_pack, LANES), F32),
            pltpu.VMEM((plane, own_pack, LANES), F32),
            pltpu.VMEM((lead, DK), BF16),
            pltpu.VMEM((reach + 1, tok, DK), BF16),
            pltpu.VMEM((reach, tok, DK), BF16),
            dma((2 * H,)),
            dma((2,)),
            dma,
            dma,
            dma((reach + 1,)),
            dma((reach + 1,)),
            dma((reach + 1,)),
            dma((hop + 1,)),
            dma,
            dma,
            dma((reach + 1,)),
            dma((reach + 1,)),
            dma((reach + 1,)),
            dma((reach + 1,)),
            dma,
            dma,
            dma,
            dma,
            dma,
            dma,
        ],
        compiler_params=pltpu.CompilerParams(
            collective_id=0, has_side_effects=True, vmem_limit_bytes=32 * 2**20
        ),
    )(
        *(
            pltpu.with_memory_space_constraint(operand, pltpu.HBM)
            for operand in (
                queries[0],
                cotangent[0],
                jnp.swapaxes(latents[0], 0, 1),
                comp_weight,
                sel_idx[0],
                sel_count,
            )
        )
    )
    return (att[None], qg[None], jnp.swapaxes(lat_grad, 0, 1)[None], weight_grad)


def solution(mesh):
    in_specs = (
        P("grp", "seq", None),
        P("grp", "seq", None),
        P("grp", "seq", None),
        P(),
        P("grp", "seq", None),
        P("grp", "seq"),
    )
    out_specs = (P("grp", "seq", None), P("grp", "seq", None), P("grp", "seq", None), P())
    return jax.shard_map(
        functools.partial(body, mesh.shape["seq"], mesh.shape["grp"]),
        mesh=mesh,
        in_specs=in_specs,
        out_specs=out_specs,
        check_vma=False,
    )
```

```python
import functools

import jax
import jax.numpy as jnp
from jax import lax
from jax.experimental import pallas as pl
from jax.experimental.pallas import tpu as pltpu
from jax.sharding import PartitionSpec as P

DL = 512
DR = 64
H = 8
QB = 64
CS = 32
WIN = 512
DK = 576
LANES = 128
WIDE = 640
PIECES = WIDE // LANES
SLOT = 8
MASKED = -1e30
UNROLL = 32
INNER = 4

MESH = pl.DeviceIdType.MESH
BF16 = jnp.bfloat16
F32 = jnp.float32
score_scale = 192.0 ** (-0.5)


def round_up(value, step):
    return (value + step - 1) // step * step


def dot_nn(a, b):
    return lax.dot_general(a, b, (((1,), (0,)), ((), ())), preferred_element_type=F32)


def dot_nt(a, b):
    return lax.dot_general(a, b, (((1,), (1,)), ((), ())), preferred_element_type=F32)


def dot_tn(a, b):
    return lax.dot_general(a, b, (((0,), (0,)), ((), ())), preferred_element_type=F32)


def piece_width(j):
    return min(LANES, DK - j * LANES)


def each(size, base, work):
    if size <= UNROLL:
        for k in range(1, size):
            work(lax.rem(base + k, size))
        return

    def one(k, c):
        work(lax.rem(base + k, size))
        return c

    lax.fori_loop(1, size, one, 0)


def kernel(
    n, groups, hop, tok, cl, inner,
    q_ref, cot_ref, lat_t_ref, cw_ref, idx_ref, cnt_ref,
    att_ref, qg_ref, lg_t_ref, wg_ref,
    lat_ref, lg_ref, qq, cc, win, comp, tmp, kk, kf, bias, ds_ref, pp, dq, att_buf, qg_buf,
    pack, cg, crecv_buf, cgrad, part, precv, lines, pout, wing, srecv, wrecv,
    load_sem, save_sem,
    gc_send, gc_recv, gw_send, gw_recv, gs_send, gs_recv,
    rc_send, rc_recv, rs_send, rs_recv, rw_send, rw_recv,
    p_send, p_recv, l_send, l_recv, o_send, o_recv,
):
    seq = lax.axis_index("seq")
    grp = lax.axis_index("grp")
    outer = n // inner
    plane = groups * inner
    depth = seq // inner
    spot = seq % inner
    rank = grp * inner + spot
    parity = seq % 2
    base = seq - parity
    sibling = base + 1 - parity
    own_rows = CS // plane
    nk = bias.shape[1]
    lead = hop * tok
    ext = lead + tok
    cp = nk - round_up(ext, LANES)
    half = (H // 2) * tok
    pair = 2 * DK
    reach = hop // 2

    def in_plane(peer):
        return (lax.div(peer, inner), depth * inner + lax.rem(peer, inner))

    def along(peer):
        return (grp, peer * inner + spot)

    def remote(src, dst, send, recv, device):
        return pltpu.make_async_remote_copy(
            src_ref=src, dst_ref=dst, send_sem=send, recv_sem=recv,
            device_id=device, device_id_type=MESH,
        )

    def wait_all(ref, sem):
        remote(ref, ref, sem, sem, (grp, sibling)).wait_recv()

    def segment(d):
        return pl.ds((hop - d) * tok, tok)

    barrier = pltpu.get_barrier_semaphore()

    def greet(device):
        pl.semaphore_signal(barrier, inc=1, device_id=device, device_id_type=MESH)

    each(n, seq, lambda peer: greet((grp, peer)))
    for g in range(1, groups):
        for i in range(inner):
            greet((lax.rem(grp + g, groups), depth * inner + i))

    loads = []
    for m in range(H // 2):
        for p in range(2):
            rows = pl.ds(p * half + m * tok, tok)
            at = 2 * (2 * m + p)
            loads.append(
                pltpu.make_async_copy(
                    q_ref.at[:, pl.ds(m * pair + p * DL, WIDE)], qq.at[rows], load_sem.at[at]
                )
            )
            loads.append(
                pltpu.make_async_copy(
                    cot_ref.at[:, pl.ds((2 * m + p) * DL, DL)], cc.at[rows], load_sem.at[at + 1]
                )
            )
    for load in loads:
        load.start()

    lat_ref[...] = lat_t_ref[...].astype(F32).T.astype(BF16)
    tmp[...] = jnp.zeros_like(tmp)
    for b in range(cl):
        block = lat_ref[pl.ds(b * CS, CS), :].astype(F32) * cw_ref[...]
        row = jnp.sum(block, axis=0, keepdims=True)
        for j in range(PIECES):
            w = piece_width(j)
            tmp[pl.ds(j * cl + b, 1), pl.ds(0, w)] = row[:, j * LANES : j * LANES + w]
    comp[seq] = tmp[...].astype(BF16)
    pl.semaphore_wait(barrier, n - 1 + (groups - 1) * inner)

    def comp_send(peer):
        return remote(comp.at[seq], comp.at[seq], gc_send, gc_recv, (grp, peer))

    def win_copy(k):
        return remote(
            lat_ref, win.at[segment(2 * k)], gw_send.at[k], gw_recv.at[k],
            (grp, (seq + 2 * k) % n),
        )

    def pass_on(k, d):
        src = lat_ref if k == 0 else win.at[segment(2 * k)]
        return remote(src, win.at[segment(d)], gs_send.at[k], gs_recv.at[d], (grp, sibling))

    def forwarded(work):
        for k in range(reach + 1):
            if k < reach:
                pl.when((parity == 0) & (base >= 2 * k))(lambda k=k: work(k, 2 * k + 1, True))
            if k > 0:
                pl.when((parity == 1) & (base >= 2 * k))(lambda k=k: work(k, 2 * k - 1, False))

    for k in range(reach, 0, -1):
        pl.when(base + 2 * k < n)(lambda k=k: win_copy(k).start())
    pl.when(parity == 0)(lambda: pass_on(0, 1).start())
    each(n, seq, lambda peer: comp_send(peer).start())

    for d in range(1, hop + 1):

        @pl.when(seq < d)
        def _(d=d):
            win[segment(d), :] = jnp.zeros((tok, DK), BF16)

    blocks = tok // QB
    slots = idx_ref.shape[1]
    key_id = lax.broadcasted_iota(jnp.int32, (cp, slots), 0)
    in_slot = key_id % SLOT
    comp_id = jnp.where(in_slot < cl, (key_id // SLOT) * cl + in_slot, -1)
    slot_id = lax.broadcasted_iota(jnp.int32, (cp, slots), 1)
    for r in range(blocks):
        chosen = idx_ref[pl.ds(r, 1), :]
        hit = (comp_id == chosen) & (slot_id < cnt_ref[0, r])
        hit = jnp.where(hit, 1.0, 0.0).astype(BF16)
        live = dot_nt(jnp.ones((QB, slots), BF16), hit)
        bias[pl.ds(r * QB, QB), pl.ds(0, cp)] = jnp.where(live > 0.5, 0.0, MASKED)
    wide = nk - cp
    row = lax.broadcasted_iota(jnp.int32, (tok, wide), 0)
    col = lax.broadcasted_iota(jnp.int32, (tok, wide), 1)
    shift = lead - WIN
    ok = (col > row + shift) & (col <= row + lead) & (col - lead + seq * tok >= 0)
    bias[:, pl.ds(cp, wide)] = jnp.where(ok, 0.0, MASKED)
    kf[pl.ds(0, cp), :] = jnp.zeros((cp, WIDE), F32)
    if nk > cp + ext:
        kk[:, pl.ds(cp + ext, nk - cp - ext), :] = jnp.zeros((2, nk - cp - ext, WIDE), BF16)

    def lay_out(d, value):
        rows = pl.ds(cp + (hop - d) * tok, tok)
        padded = jnp.concatenate(
            [value.astype(F32), jnp.zeros((tok, WIDE - DK), F32)], axis=1
        )
        kk[0, rows, :] = padded.astype(BF16)
        kk[1, rows, :] = pltpu.roll(padded, DR, 1).astype(BF16)

    lay_out(0, lat_ref[...])
    pack[...] = jnp.zeros_like(pack)
    part[...] = jnp.zeros_like(part)

    for k in range(1, reach + 1):

        @pl.when(base >= 2 * k)
        def _(k=k):
            win_copy(k).wait_recv()
            if k < reach:
                pl.when(parity == 0)(lambda: pass_on(k, 2 * k + 1).start())
            pl.when(parity == 1)(lambda: pass_on(k, 2 * k - 1).start())

    for k in range(1, reach + 1):
        lay_out(2 * k, win[segment(2 * k), :])
    wait_all(comp.at[pl.ds(0, n - 1)], gc_recv)

    def unpack(o, c):
        packed = comp[o].astype(F32)
        for j in range(PIECES):
            kf[pl.ds(pl.multiple_of(o * SLOT, SLOT), cl), pl.ds(j * LANES, LANES)] = packed[
                j * cl : (j + 1) * cl, :
            ]
        return c

    lax.fori_loop(0, n, unpack, 0)
    kk[0, pl.ds(0, cp), :] = kf[pl.ds(0, cp), :].astype(BF16)
    kk[1, pl.ds(0, cp), :] = pltpu.roll(kf[pl.ds(0, cp), :], DR, 1).astype(BF16)

    def sibling_arrival(k, d):
        pass_on(k, d).wait_recv()

    for k in range(reach + 1):
        if k < reach:
            pl.when((parity == 1) & (base >= 2 * k))(lambda k=k: sibling_arrival(k, 2 * k + 1))
        if k > 0:
            pl.when((parity == 0) & (base >= 2 * k))(lambda k=k: sibling_arrival(k, 2 * k - 1))
    for d in range(1, hop + 1, 2):
        lay_out(d, win[segment(d), :])
    for load in loads:
        load.wait()

    step = min(256, half)
    heads = step // tok
    for c in range(2 * half // step):
        p = c * step // half
        rows = pl.ds(c * step, step)
        keys = kk[p]
        values = kk[0, :, pl.ds(0, DL)]
        s = dot_nt(qq[rows, :], keys) * score_scale
        s = (s.reshape(heads, tok, nk) + bias[...][None]).reshape(step, nk)
        e = jnp.exp(s - jnp.max(s, axis=1, keepdims=True))
        w = e * (1.0 / jnp.sum(e, axis=1, keepdims=True))
        rounded = w.astype(BF16)
        pp[rows, :] = rounded
        context = dot_nn(rounded, values)
        grads = cc[rows, :]
        row_dot = jnp.sum(grads.astype(F32) * context, axis=1, keepdims=True)
        dscore = (w * (dot_nt(grads, values) - row_dot)).astype(BF16)
        ds_ref[rows, :] = dscore
        dq[rows, :] = dot_nn(dscore, keys) * score_scale
        for i in range(heads):
            m = (c * step - p * half) // tok + i
            att_buf[:, pl.ds((2 * m + p) * DL, DL)] = context[i * tok : (i + 1) * tok].astype(BF16)

    save_att = pltpu.make_async_copy(att_buf, att_ref, save_sem.at[0])
    save_att.start()

    def key_pass(start, stop):
        size = min(256, stop - start)
        cols = pl.ds(start, size)
        even = dot_tn(ds_ref[pl.ds(0, half), cols], qq[pl.ds(0, half), :])
        odd = dot_tn(ds_ref[pl.ds(half, half), cols], qq[pl.ds(half, half), :])
        value = dot_tn(pp[:, cols], cc[...])
        total = (even + pltpu.roll(odd, WIDE - DR, 1)) * score_scale
        kf[cols, pl.ds(0, DL)] = total[:, :DL] + value
        kf[cols, pl.ds(DL, LANES)] = total[:, DL:]

    def seg_grad(d):
        return kf[pl.ds(cp + (hop - d) * tok, tok), pl.ds(0, DK)]

    def sum_send(peer):
        return remote(cg.at[peer], crecv_buf.at[seq], rc_send, rc_recv, (grp, peer))

    def to_sibling(k, d):
        return remote(
            wing.at[segment(d)], srecv.at[k], rs_send.at[k], rs_recv.at[k], (grp, sibling)
        )

    def to_source(k):
        return remote(
            wing.at[segment(2 * k)], wrecv.at[k - 1], rw_send.at[k], rw_recv.at[k],
            (grp, (seq + n - 2 * k) % n),
        )

    def part_copy(peer):
        return remote(part.at[peer], precv.at[rank], p_send, p_recv, in_plane(peer))

    def line_copy(peer):
        return remote(lines.at[depth], lines.at[depth], l_send, l_recv, along(peer))

    def out_copy(peer):
        return remote(pout.at[rank], pout.at[rank], o_send, o_recv, in_plane(peer))

    done = 0
    while done < cp:
        key_pass(done, cp)
        done = min(done + 256, cp)

    def pack_one(o, c):
        for j in range(PIECES):
            pack[o, pl.ds(j * cl, cl), :] = kf[
                pl.ds(pl.multiple_of(o * SLOT, SLOT), cl), pl.ds(j * LANES, LANES)
            ]
        return c

    lax.fori_loop(0, n, pack_one, 0)
    cg[...] = pack[...].astype(BF16)
    crecv_buf[seq] = cg[seq]
    each(n, seq, lambda peer: sum_send(peer).start())

    def send_sibling(k, d):
        wing[segment(d), :] = seg_grad(d).astype(BF16)
        to_sibling(k, d).start()

    def back(work):
        for k in range(reach, -1, -1):
            if k > 0:
                pl.when((parity == 0) & (base >= 2 * k))(lambda k=k: work(k, 2 * k - 1, True))
            if k < reach:
                pl.when((parity == 1) & (base >= 2 * k))(lambda k=k: work(k, 2 * k + 1, False))

    def ship(d):
        if d == hop:

            @pl.when((parity == 0) & (base >= hop))
            def _():
                wing[segment(hop), :] = seg_grad(hop).astype(BF16)
                to_source(reach).start()

        elif d % 2 == 1:
            k = (d + 1) // 2
            pl.when((parity == 0) & (base >= 2 * k))(lambda: send_sibling(k, d))
            pl.when((parity == 1) & (base >= 2 * k - 2))(lambda: send_sibling(k - 1, d))

    ready = hop
    while True:
        while ready > 0 and cp + (hop - ready + 1) * tok <= done:
            ship(ready)
            ready -= 1
        if done >= nk:
            break
        key_pass(done, nk)
        done = min(done + 256, nk)

    wait_all(crecv_buf.at[pl.ds(0, n - 1)], rc_recv)
    total = jnp.sum(crecv_buf[...].astype(F32), axis=0)
    for j in range(PIECES):
        cgrad[pl.ds(0, cl), pl.ds(j * LANES, LANES)] = total[j * cl : (j + 1) * cl, :]
    weight = jnp.zeros((CS, DK), F32)
    for b in range(cl):
        weight = weight + cgrad[pl.ds(b, 1), pl.ds(0, DK)] * lat_ref[pl.ds(b * CS, CS), :].astype(F32)
    for o in range(plane):
        for j in range(PIECES):
            w = piece_width(j)
            part[o, pl.ds(j * own_rows, own_rows), pl.ds(0, w)] = weight[
                o * own_rows : (o + 1) * own_rows, j * LANES : j * LANES + w
            ]
    each(plane, rank, lambda peer: part_copy(peer).start())
    precv[rank] = part[rank]

    def merge(k):
        to_sibling(k, 1).wait_recv()
        wing[segment(2 * k), :] = (seg_grad(2 * k) + srecv[k].astype(F32)).astype(BF16)
        to_source(k).start()

    for k in range(reach, 0, -1):
        if k < reach:
            pl.when(base >= 2 * k)(lambda k=k: merge(k))
        else:
            pl.when((parity == 1) & (base >= 2 * k))(lambda k=k: merge(k))

    wait_all(precv.at[pl.ds(0, plane - 1)], p_recv)
    lines[depth] = jnp.sum(precv[...], axis=0)
    each(outer, depth, lambda peer: line_copy(peer).start())

    wait_all(lines.at[pl.ds(0, outer - 1)], l_recv)
    pout[rank] = jnp.sum(lines[...], axis=0)
    each(plane, rank, lambda peer: out_copy(peer).start())

    for m in range(H // 2):
        even = pl.ds(m * tok, tok)
        odd = pl.ds(half + m * tok, tok)
        qg_buf[:, pl.ds(m * pair, DL)] = dq[even, pl.ds(0, DL)].astype(BF16)
        qg_buf[:, pl.ds(m * pair + DL, LANES)] = (
            dq[even, pl.ds(DL, LANES)] + dq[odd, pl.ds(0, LANES)]
        ).astype(BF16)
        qg_buf[:, pl.ds(m * pair + WIDE, DL)] = dq[odd, pl.ds(LANES, DL)].astype(BF16)
    save_qg = pltpu.make_async_copy(qg_buf, qg_ref, save_sem.at[1])
    save_qg.start()

    own = seg_grad(0)
    for b in range(cl):
        rows = pl.ds(b * CS, CS)
        lg_ref[rows, :] = own[b * CS : (b + 1) * CS] + cw_ref[...] * cgrad[pl.ds(b, 1), pl.ds(0, DK)]

    @pl.when(parity == 0)
    def _():
        to_sibling(0, 1).wait_recv()
        lg_ref[...] += srecv[0].astype(F32)

    for k in range(1, reach + 1):

        @pl.when(base + 2 * k < n)
        def _(k=k):
            to_source(k).wait_recv()
            lg_ref[...] += wrecv[k - 1].astype(F32)

    lg_t_ref[...] = lg_ref[...].T
    wait_all(pout.at[pl.ds(0, plane - 1)], o_recv)
    for o in range(plane):
        for j in range(PIECES):
            w = piece_width(j)
            wg_ref[pl.ds(o * own_rows, own_rows), pl.ds(j * LANES, w)] = pout[
                o, pl.ds(j * own_rows, own_rows), pl.ds(0, w)
            ]

    save_att.wait()
    save_qg.wait()
    wait_all(comp.at[pl.ds(0, n - 1)], gc_send)
    wait_all(cg.at[pl.ds(0, n - 1)], rc_send)
    for k in range(1, reach + 1):
        pl.when(base + 2 * k < n)(lambda k=k: win_copy(k).wait_send())
        pl.when(base >= 2 * k)(lambda k=k: to_source(k).wait_send())
    forwarded(lambda k, d, unused: pass_on(k, d).wait_send())
    back(lambda k, d, unused: to_sibling(k, d).wait_send())
    wait_all(part.at[pl.ds(0, plane - 1)], p_send)
    wait_all(lines.at[pl.ds(0, outer - 1)], l_send)
    wait_all(pout.at[pl.ds(0, plane - 1)], o_send)


def body(n, groups, queries, latents, cotangent, comp_weight, sel_idx, sel_count):
    tok = latents.shape[1]
    hop = (WIN + tok - 1) // tok
    assert hop % 2 == 0 and n % 2 == 0
    lead = hop * tok
    cl = tok // CS
    pr = round_up(cl * PIECES, 16)
    nk = round_up(n * SLOT, LANES) + round_up(lead + tok, LANES)
    inner = INNER
    plane = groups * inner
    assert n % inner == 0 and CS % plane == 0
    own_pack = round_up(CS // plane * PIECES, SLOT)
    dma = pltpu.SemaphoreType.DMA
    reach = hop // 2
    any_spec = pl.BlockSpec(memory_space=pl.ANY)
    hbm_spec = pl.BlockSpec(memory_space=pltpu.HBM)
    vmem_spec = pl.BlockSpec(memory_space=pltpu.VMEM)
    att, qg, lat_grad, weight_grad = pl.pallas_call(
        functools.partial(kernel, n, groups, hop, tok, cl, inner),
        out_shape=(
            jax.ShapeDtypeStruct((tok, H * DL), BF16),
            jax.ShapeDtypeStruct((tok, H * DK), BF16),
            jax.ShapeDtypeStruct((DK, tok), F32),
            jax.ShapeDtypeStruct((CS, DK), F32),
        ),
        in_specs=[
            hbm_spec,
            hbm_spec,
            vmem_spec,
            vmem_spec,
            vmem_spec,
            pl.BlockSpec(memory_space=pltpu.SMEM),
        ],
        out_specs=(any_spec, any_spec, vmem_spec, vmem_spec),
        scratch_shapes=[
            pltpu.VMEM((tok, DK), BF16),
            pltpu.VMEM((tok, DK), F32),
            pltpu.VMEM((H * tok, WIDE), BF16),
            pltpu.VMEM((H * tok, DL), BF16),
            pltpu.VMEM((lead, DK), BF16),
            pltpu.VMEM((n, pr, LANES), BF16),
            pltpu.VMEM((pr, LANES), F32),
            pltpu.VMEM((2, nk, WIDE), BF16),
            pltpu.VMEM((nk, WIDE), F32),
            pltpu.VMEM((tok, nk), F32),
            pltpu.VMEM((H * tok, nk), BF16),
            pltpu.VMEM((H * tok, nk), BF16),
            pltpu.VMEM((H * tok, WIDE), F32),
            pltpu.VMEM((tok, H * DL), BF16),
            pltpu.VMEM((tok, H * DK), BF16),
            pltpu.VMEM((n, pr, LANES), F32),
            pltpu.VMEM((n, pr, LANES), BF16),
            pltpu.VMEM((n, pr, LANES), BF16),
            pltpu.VMEM((SLOT, WIDE), F32),
            pltpu.VMEM((plane, own_pack, LANES), F32),
            pltpu.VMEM((plane, own_pack, LANES), F32),
            pltpu.VMEM((n // inner, own_pack, LANES), F32),
            pltpu.VMEM((plane, own_pack, LANES), F32),
            pltpu.VMEM((lead, DK), BF16),
            pltpu.VMEM((reach + 1, tok, DK), BF16),
            pltpu.VMEM((reach, tok, DK), BF16),
            dma((2 * H,)),
            dma((2,)),
            dma,
            dma,
            dma((reach + 1,)),
            dma((reach + 1,)),
            dma((reach + 1,)),
            dma((hop + 1,)),
            dma,
            dma,
            dma((reach + 1,)),
            dma((reach + 1,)),
            dma((reach + 1,)),
            dma((reach + 1,)),
            dma,
            dma,
            dma,
            dma,
            dma,
            dma,
        ],
        compiler_params=pltpu.CompilerParams(
            collective_id=0, has_side_effects=True, vmem_limit_bytes=32 * 2**20
        ),
    )(
        *(
            pltpu.with_memory_space_constraint(operand, pltpu.HBM)
            for operand in (
                queries[0],
                cotangent[0],
                jnp.swapaxes(latents[0], 0, 1),
                comp_weight,
                sel_idx[0],
                sel_count,
            )
        )
    )
    return (att[None], qg[None], jnp.swapaxes(lat_grad, 0, 1)[None], weight_grad)


def solution(mesh):
    in_specs = (
        P("grp", "seq", None),
        P("grp", "seq", None),
        P("grp", "seq", None),
        P(),
        P("grp", "seq", None),
        P("grp", "seq"),
    )
    out_specs = (P("grp", "seq", None), P("grp", "seq", None), P("grp", "seq", None), P())
    return jax.shard_map(
        functools.partial(body, mesh.shape["seq"], mesh.shape["grp"]),
        mesh=mesh,
        in_specs=in_specs,
        out_specs=out_specs,
        check_vma=False,
    )
```
